128 devices in a mesh: pix: 64 (over x, z, y_lo, core), ch: 2 (over y_hi).
Axes of the slice: x: 4, y: 4 (y_hi: 2, y_lo: 2; y = y_hi * 2 + y_lo), z: 4, core: 2. Of those that a mesh axis runs over, the one named last changes fastest.
Arguments:
- features: bfloat16 [32, 2048, 2048], P(None, 'pix'), may hold values from -6 to 6
- grad_out: bfloat16 [32, 2048, 2048], P('ch', 'pix'), may hold values from -6 to 6
- cheb_weight: bfloat16 [4, 32, 32], P(None, None, 'ch'), may hold values from -0.5 to 0.5
- east_weight: float32 [2048, 2048], P('pix'), may hold values from 0.05 to 0.25
- south_weight: float32 [2048, 2048], P('pix'), may hold values from 0.05 to 0.25
- pixel_mask: int32 [2048, 2048], P('pix'), may hold values 0 or 1
Outputs:
- input_grad: bfloat16 [32, 2048, 2048], P('ch', 'pix')
- weight_grad: float32 [4, 32, 32], P(None, None, 'ch')
The draws below stay inside these ranges and needn't reach their ends.
All inputs are finite; a program needn't handle non-finite values. No bound on the sum of `pixel_mask` on one device may be relied on, other than what follows from the above.
Results may differ from the reference program's by a relative error of at most 0.006.
Values may be sent and summed in bfloat16 or wider, within the bound.
No kernel may reach another device: no remote copies, remote signals or barrier semaphores. Data moves between devices by JAX's collectives and lax.ppermute only.
A program may use at most 128 MiB of HBM per device.

```python
import jax
import jax.numpy as jnp

CIN = 32
COUT = 32
KTERMS = 4
NSIDE = 2048
PIXROWS = 2048
PIXELS = 4194304


def with_ends(array, own_key, low, top_value):
    longest = array.shape.index(max(array.shape))
    spots = []
    for shift in (0, 1):
        where = [jax.random.randint(jax.random.fold_in(own_key, axis), (), 0, length) for axis, length in enumerate(array.shape)]
        where[longest] = (where[longest] + shift) % array.shape[longest]
        spots.append(tuple(where))
    return array.at[spots[0]].set(low).at[spots[1]].set(top_value)


def shard_levels(stream_key, dims, shards, low, high):
    def one(dim, parts):
        steps = jax.random.uniform(jax.random.fold_in(jax.random.fold_in(stream_key, 6), dim), (parts,), jnp.float32, low / len(shards), high / len(shards))
        return jnp.repeat(jnp.exp(steps), dims[dim] // parts).reshape((-1,) + (1,) * (len(dims) - dim - 1))

    gain = one(*shards[0])
    for cut in shards[1:]:
        gain = gain * one(*cut)
    return gain


def normal_values(rng, extent, spread, reach, cuts=(), kind=jnp.bfloat16):
    factor_of = shard_levels(rng, extent, cuts, -0.22, 0.18) if cuts else 1.0
    result = jax.random.normal(rng, extent, jnp.float32) * spread * factor_of
    return jnp.minimum(jnp.maximum(result, -reach), reach).astype(kind)


def setup_inputs(seed: int = 0) -> dict:
    splits = jax.random.split(jax.random.key(seed), 7)
    features = normal_values(splits[0], (CIN, PIXROWS, NSIDE), 1.0, 6.0, ((1, 64),))
    grad_out = normal_values(splits[1], (COUT, PIXROWS, NSIDE), 1.0, 6.0, ((0, 2), (1, 64)))
    cheb_weight = normal_values(splits[2], (KTERMS, CIN, COUT), (KTERMS * COUT) ** -0.5, 0.5, ((2, 2),))
    east_weight = jnp.clip(0.05 + 0.2 * jax.random.uniform(splits[3], (PIXROWS, NSIDE), jnp.float32) ** shard_levels(splits[3], (PIXROWS, NSIDE), ((0, 64),), -0.2, 0.2), 0.05, 0.25)
    south_weight = jnp.clip(0.05 + 0.2 * jax.random.uniform(splits[4], (PIXROWS, NSIDE), jnp.float32) ** shard_levels(splits[4], (PIXROWS, NSIDE), ((0, 64),), -0.2, 0.2), 0.05, 0.25)
    pixel_mask = with_ends((jax.random.randint(splits[5], (PIXROWS, NSIDE), 0, 8) < 7).astype(jnp.int32), jax.random.fold_in(splits[5], 1), 0, 1)
    return dict(features=features, grad_out=grad_out, cheb_weight=cheb_weight, east_weight=east_weight, south_weight=south_weight, pixel_mask=pixel_mask)


def edge_weights(east_weight, south_weight, pixel_mask):
    maskf = pixel_mask.astype(jnp.float32)
    columns = jnp.arange(NSIDE)
    rownum = jnp.arange(PIXROWS)
    mask_right = jnp.concatenate([maskf[:, 1:], jnp.zeros((PIXROWS, 1), jnp.float32)], axis=1)
    east_eff = east_weight * maskf * mask_right * (columns < NSIDE - 1).astype(jnp.float32)[None, :]
    mask_down = jnp.concatenate([maskf[1:], jnp.zeros((1, NSIDE), jnp.float32)], axis=0)
    face_keep = ((rownum + 1) % NSIDE != 0).astype(jnp.float32)[:, None]
    south_eff = south_weight * maskf * mask_down * face_keep
    west_eff = jnp.concatenate([jnp.zeros((PIXROWS, 1), jnp.float32), east_eff[:, :-1]], axis=1)
    north_eff = jnp.concatenate([jnp.zeros((1, NSIDE), jnp.float32), south_eff[:-1]], axis=0)
    return (east_eff, west_eff, south_eff, north_eff)

def operate(field, wts):
    east_eff, west_eff, south_eff, north_eff = wts
    chans = field.shape[0]
    zcol = jnp.zeros((chans, field.shape[1], 1), jnp.float32)
    zrow = jnp.zeros((chans, 1, field.shape[2]), jnp.float32)
    right = jnp.concatenate([field[:, :, 1:], zcol], axis=2)
    left = jnp.concatenate([zcol, field[:, :, :-1]], axis=2)
    below = jnp.concatenate([field[:, 1:], zrow], axis=1)
    above = jnp.concatenate([zrow, field[:, :-1]], axis=1)
    return -(east_eff * right + west_eff * left + south_eff * below + north_eff * above)

def reference(features, grad_out, cheb_weight, east_weight, south_weight, pixel_mask):
    wts = edge_weights(east_weight, south_weight, pixel_mask)
    grad32 = grad_out.astype(jnp.float32)
    grads = []
    prev_term = None
    term_now = features.astype(jnp.float32)
    for order in range(KTERMS):
        if order == 1:
            prev_term, term_now = (term_now, operate(term_now, wts))
        elif order > 1:
            prev_term, term_now = (term_now, 2.0 * operate(term_now, wts) - prev_term)
        term_b = term_now.astype(jnp.bfloat16).astype(jnp.float32)
        grads.append(jnp.einsum('irn,orn->io', term_b, grad32))
    weight_grad = jnp.stack(grads) / jnp.sqrt(jnp.float32(PIXELS))
    weight32 = cheb_weight.astype(jnp.float32)

    def part(order):
        return jnp.einsum('io,orn->irn', weight32[order], grad32)
    clen = part(KTERMS - 1)
    clen_next = jnp.zeros_like(clen)
    for order in range(KTERMS - 2, 0, -1):
        clen, clen_next = (part(order) + 2.0 * operate(clen, wts) - clen_next, clen)
    input_grad = (part(0) + operate(clen, wts) - clen_next).astype(jnp.bfloat16)
    return (input_grad, weight_grad)
```

```python
import functools

import jax
import jax.numpy as jnp
from jax import lax
from jax.experimental import pallas as pl
from jax.experimental.pallas import tpu as pltpu
from jax.sharding import PartitionSpec as P

HALO = 4
SIDE = 128
SUB = 16
TILE = 8
INNER = (512, 1536)
OUTER = (1024, 1024)
UNIT = 256
ANY = pl.BlockSpec(memory_space=pl.ANY)
HBM = pl.BlockSpec(memory_space=pltpu.HBM)
VMEM = pl.BlockSpec(memory_space=pltpu.VMEM)
F32, BF16 = jnp.float32, jnp.bfloat16


def params(mib):
    return pltpu.CompilerParams(vmem_limit_bytes=mib * 1024 * 1024)


COST = pl.CostEstimate(flops=1, bytes_accessed=1, transcendentals=0)
LONG = pl.CostEstimate(flops=10**10, bytes_accessed=10**8, transcendentals=0)


def iota(shape, dim):
    return lax.broadcasted_iota(jnp.int32, shape, dim)


def prepare_kernel(
    sides, w_hbm, g_ref, east_ref, south_ref, mask_ref,
    mix_ref, g_out, maps_out, top_ref, bottom_ref, mask_buf, w_ref, sems,
):
    copies = [
        pltpu.make_async_copy(src, dst, sems.at[n])
        for n, (src, dst) in enumerate((
            (w_hbm, w_ref), (mask_ref, mask_buf), (east_ref, maps_out.at[0]),
            (south_ref, maps_out.at[1]), (g_ref, g_out),
        ))
    ]
    for c in copies:
        c.start()
    copies[0].wait()
    nterms, nout, nin = w_ref.shape
    rows, cols = nin * SUB, nout * SUB
    part = nin // sides
    first = (lax.axis_index("ch") + 1) * part
    source = lax.rem(iota((rows, nin), 0) // SUB + first, nin)
    left = (source == iota((rows, nin), 1)).astype(BF16)
    right = (iota((nout, cols), 0) == iota((nout, cols), 1) // SUB).astype(BF16)
    keep = iota((rows, cols), 0) % SUB == iota((rows, cols), 1) % SUB
    for k in range(nterms):
        tall = lax.dot_general(
            left, w_ref[k], (((1,), (1,)), ((), ())), preferred_element_type=F32
        ).astype(BF16)
        full = jnp.dot(tall, right, preferred_element_type=F32)
        mix_ref[:, k * cols : (k + 1) * cols] = jnp.where(keep, full, 0.0).astype(BF16)
    for c in copies[1:4]:
        c.wait()
    mask = mask_buf[...].astype(F32)
    height, total = mask.shape
    east = -2.0 * maps_out[0] * mask * pltpu.roll(mask, total - 1, 1)
    maps_out[0] = jnp.where(iota(mask.shape, 1) == total - 1, 0.0, east)
    maps_out[2] = mask
    copies[4].wait()
    nch = g_out.shape[0]
    for o in range(nch + 3):
        x = g_out[o].astype(F32) if o < nch else maps_out[o - nch]
        top_ref[o] = x[:HALO].astype(BF16)
        bottom_ref[o] = x[height - TILE :][TILE - HALO :].astype(BF16)


def prepare(w, g, east, south, mask, sides):
    nterms, nin, nout = w.shape
    nch, rows, total = g.shape
    edge = jax.ShapeDtypeStruct((nch + 3, HALO, total), BF16)
    args = (w.transpose(0, 2, 1), g, east, south, mask)
    return pl.pallas_call(
        functools.partial(prepare_kernel, sides),
        out_shape=(
            jax.ShapeDtypeStruct((nin * SUB, nterms * nout * SUB), BF16),
            jax.ShapeDtypeStruct(g.shape, g.dtype),
            jax.ShapeDtypeStruct((3, rows, total), F32),
            edge,
            edge,
        ),
        in_specs=[HBM] * 5,
        out_specs=[VMEM] * 5,
        scratch_shapes=[
            pltpu.VMEM((rows, total), jnp.int32),
            pltpu.VMEM((nterms, nout, nin), BF16),
            pltpu.SemaphoreType.DMA((5,)),
        ],
        compiler_params=params(12),
        cost_estimate=COST,
    )(*(pltpu.with_memory_space_constraint(x, pltpu.HBM) for x in args))


def inner_rows(x):
    rows = x.shape[0]
    low = iota((TILE, x.shape[1]), 0) < HALO
    return jnp.concatenate(
        [x[TILE : rows - TILE], jnp.where(low, x[rows - TILE :], x[:TILE])], axis=0
    )


def outer_rows(x, below, above):
    rows = x.shape[0]
    low = iota((TILE, x.shape[1]), 0) < HALO
    return jnp.concatenate(
        [
            x[rows - TILE :], below, above, x[:TILE],
            jnp.where(low, x[TILE : 2 * TILE], x[rows - 2 * TILE : rows - TILE]),
        ],
        axis=0,
    )


def terms_kernel(outer, off, lo, hi, nterms, waits, *refs):
    g_ref, maps_ref, mix_ref = refs[waits : waits + 3]
    below_ref, above_ref = refs[waits + 3 : waits + 5] if outer else (None, None)
    terms_ref, send_ref, w_buf = refs[-3:]
    nch = g_ref.shape[0]
    ext, span = w_buf.shape[1:]
    width = terms_ref.shape[2]
    cols = slice(lo, hi)

    def arrange(x, n):
        x = x.astype(F32)
        if outer:
            below, above = below_ref[n, :, cols], above_ref[n, :, cols]
            return outer_rows(x, below.astype(F32), above.astype(F32))
        return inner_rows(x)

    ew = arrange(maps_ref[0, :, cols], nch)
    south = arrange(maps_ref[1, :, cols], nch + 1)
    mask = arrange(maps_ref[2, :, cols], nch + 2)
    row, col = iota((ext, span), 0), iota((ext, span), 1)
    ww = pltpu.roll(ew, 1, 1)
    if lo == 0:
        ww = jnp.where(col == 0, 0.0, ww)
    sw = -2.0 * south * mask * pltpu.roll(mask, ext - 1, 0)
    for gap in (TILE + HALO - 1, 3 * TILE + HALO - 1) if outer else (ext - HALO - 1,):
        sw = jnp.where(row == gap, 0.0, sw)
    w_buf[0] = ew
    w_buf[1] = ww
    w_buf[2] = sw
    w_buf[3] = pltpu.roll(sw, 1, 0)

    def twice(fields, rounded):
        east, west, south, north = (w_buf[n] for n in range(4))
        out = []
        for v, b in zip(fields, rounded):
            right = pltpu.roll(b, span - 1, 1).astype(F32)
            left = pltpu.roll(b, 1, 1).astype(F32)
            out.append(
                (east * right + west * left)
                + (south * pltpu.roll(v, ext - 1, 0) + north * pltpu.roll(v, 1, 0))
            )
        return out

    def keep(v):
        v = v[:, off : off + width]
        if outer:
            v = jnp.concatenate([v[:TILE], v[2 * TILE : 3 * TILE]], axis=0)
        return v[:SUB].astype(BF16)

    group = 4

    def channels(step, carry):
        chans = [step * group + n for n in range(group)]
        now = [arrange(g_ref[o, :, cols], o) for o in chans]
        prev = None
        for k in range(nterms):
            if k > 0:
                new = twice(now, rounded)
                new = [0.5 * x for x in new] if k == 1 else [x - p for x, p in zip(new, prev)]
                prev, now = now, new
            rounded = [x.astype(BF16) for x in now]
            for o, x in zip(chans, now):
                terms_ref[k * nch + o] = keep(x)
        return carry

    lax.fori_loop(0, nch // group, channels, 0)
    for c in range(0, width, 256):
        x = terms_ref[:, :, c : c + 256].reshape(nterms * nch * SUB, 256)
        y = jnp.dot(mix_ref[: send_ref.shape[0] * SUB], x, preferred_element_type=F32)
        send_ref[:, :, c : c + 256] = y.astype(BF16).reshape(-1, SUB, 256)


def chunk_terms(outer, start, width, g, maps, mix, sent, nterms, beside, waits, cost):
    nch, rows, total = g.shape
    lo, hi = max(0, start - SIDE), min(total, start + width + SIDE)
    ext = 4 * TILE if outer else 3 * TILE
    return pl.pallas_call(
        functools.partial(terms_kernel, outer, start - lo, lo, hi, nterms, len(waits)),
        out_shape=(
            jax.ShapeDtypeStruct((nterms * nch, SUB, width), BF16),
            jax.ShapeDtypeStruct((sent, SUB, width), BF16),
        ),
        in_specs=[ANY] * len(waits) + [VMEM] * (3 + len(beside)),
        out_specs=(VMEM, VMEM),
        scratch_shapes=[pltpu.VMEM((4, ext, hi - lo), F32)],
        compiler_params=params(20),
        cost_estimate=cost,
    )(*waits, g, maps, mix, *beside)


def weights_kernel(places, f_ref, *refs):
    n = len(places)
    terms, (grad_ref, acc) = refs[:n], refs[n:]
    nt = terms[0].shape[0]
    nin, rows, _ = f_ref.shape
    for m, ((outer, start, width), t_ref) in enumerate(zip(places, terms)):
        x = t_ref[...].reshape(nt * SUB, width)
        f = f_ref[:, :, start : start + width].astype(F32)
        if outer:
            f = jnp.concatenate([f[:, rows - TILE :], f[:, :TILE]], axis=1)
        else:
            f = f[:, TILE : rows - TILE]
        f = f.astype(BF16).reshape(nin * SUB, width)
        y = lax.dot_general(x, f, (((1,), (1,)), ((), ())), preferred_element_type=F32)
        if m == 0:
            acc[...] = y
        else:
            acc[...] += y
    r, c = iota((SUB, nin * SUB), 0), iota((SUB, nin * SUB), 1)
    same = (c % SUB == r).astype(F32)
    kept = jnp.sum(acc[...].reshape(nt, SUB, nin * SUB) * same[None], axis=1)
    pick = (iota((nin * SUB, nin), 0) // SUB == iota((nin * SUB, nin), 1)).astype(F32)
    grad_ref[...] = jnp.dot(
        kept, pick, preferred_element_type=F32, precision=lax.Precision.HIGHEST
    )


def weights(places, terms, f):
    nt = terms[0].shape[0]
    nin = f.shape[0]
    return pl.pallas_call(
        functools.partial(weights_kernel, places),
        out_shape=jax.ShapeDtypeStruct((nt, nin), F32),
        in_specs=[VMEM] * (1 + len(terms)),
        out_specs=VMEM,
        scratch_shapes=[pltpu.VMEM((nt * SUB, nin * SUB), F32)],
        compiler_params=params(36),
        cost_estimate=COST,
    )(f, *terms)


def finish_kernel(mix_ref, terms_i, got_i, terms_o, got_o, *refs):
    out = []
    for terms, got in ((terms_i, got_i), (terms_o, got_o)):
        x = terms[...].reshape(-1, UNIT)
        own = jnp.dot(mix_ref[...], x, preferred_element_type=F32)
        out.append(own.reshape(got.shape) + got[...].astype(F32))
    inner, outer = out
    refs[-1][...] = jnp.concatenate([outer[:, TILE:], inner, outer[:, :TILE]], axis=1).astype(BF16)


def finish(start, width, mix, inner, outer, out, rows, total):
    kept = outer[2].shape[0]
    nt = outer[1].shape[0]
    extra = () if out is None else (out,)
    last = mix.shape[0] // (kept * SUB) - 1

    def blocks(piece):
        def index(j):
            return (0, 0, j + (start - piece[0]) // UNIT)

        return [pl.BlockSpec((n, SUB, UNIT), index) for n in (nt, kept)]

    return pl.pallas_call(
        finish_kernel,
        grid=(width // UNIT,),
        out_shape=jax.ShapeDtypeStruct((kept, rows, total), BF16),
        in_specs=[pl.BlockSpec((kept * SUB, mix.shape[1]), lambda j: (last, 0))]
        + blocks(inner)
        + blocks(outer)
        + [ANY] * len(extra),
        out_specs=pl.BlockSpec((kept, rows, UNIT), lambda j: (0, 0, j + start // UNIT)),
        input_output_aliases={5: 0} if extra else {},
        compiler_params=params(16),
        cost_estimate=COST,
    )(mix, *inner[1:], *outer[1:], *extra)


def add_kernel(count, *refs):
    values = [r[...] for r in refs[:count]]
    while len(values) > 1:
        values = [a + b for a, b in zip(values[::2], values[1::2])]
    refs[-1][...] = values[0]


def add(values, waits):
    return pl.pallas_call(
        functools.partial(add_kernel, len(values)),
        out_shape=jax.ShapeDtypeStruct(values[0].shape, F32),
        in_specs=[VMEM] * len(values) + [ANY] * len(waits),
        out_specs=VMEM,
        compiler_params=params(4),
        cost_estimate=COST,
    )(*values, *waits)


def sum_over_pix(value, size, waits):
    steps, step = [], 1
    while step < size:
        steps.append((step, 4 if step * 2 < size else 2))
        step *= steps[-1][1]
    value = add([value], waits[0])
    for n, (step, count) in enumerate(steps[1:] + steps[:1]):
        moved = [
            lax.ppermute(value, "pix", [(i, i ^ (x * step)) for i in range(size)])
            for x in range(1, count)
        ]
        value = add([value, *moved], waits[n + 1] if n + 1 < len(waits) else ())
    return value


def per_device(features, grad_out, cheb_weight, east_weight, south_weight, pixel_mask):
    nch, rows, total = grad_out.shape
    nterms, nin, _ = cheb_weight.shape
    size, sides = lax.axis_size("pix"), lax.axis_size("ch")
    part = nin // sides
    mix, g, maps, top, bottom = prepare(
        cheb_weight, grad_out, east_weight, south_weight, pixel_mask, sides
    )
    pieces = []

    def chunks(outer, widths, beside):
        start = 0
        for width in widths:
            waits = [pieces[-1][1]] if pieces else []
            waits += [pieces[0][2]] if outer and not start else []
            cost = LONG if outer and not start else COST
            terms, send = chunk_terms(
                outer, start, width, g, maps, mix, part, nterms, beside, waits, cost
            )
            got = lax.ppermute(send, "ch", [(i, i ^ 1) for i in range(sides)])
            pieces.append(((outer, start, width), terms, got))
            start += width

    chunks(False, INNER, ())
    down = [(i, i + 1) for i in range(size - 1) if (i + 1) * rows % total]
    up = [(j, i) for i, j in down]
    chunks(True, OUTER, (lax.ppermute(top, "pix", up), lax.ppermute(bottom, "pix", down)))

    grad = weights([p[0] for p in pieces], [p[1] for p in pieces], features)
    pixels = rows * size * total
    arrived = [got for _, _, got in pieces]
    n = len(INNER)
    grad = sum_over_pix(grad, size, (arrived[:n], arrived[n:-1])) / jnp.sqrt(F32(pixels))
    weight_grad = grad.reshape(nterms, nch, nin).transpose(0, 2, 1)
    out = None
    for (_, at, width), outer_terms, outer_got in pieces[n:]:
        for (_, first, span), inner_terms, inner_got in pieces[:n]:
            lo, hi = max(at, first), min(at + width, first + span)
            if lo < hi:
                inner = (first, inner_terms, inner_got)
                outer = (at, outer_terms, outer_got)
                out = finish(lo, hi - lo, mix, inner, outer, out, rows, total)
    return out, weight_grad


def solution(mesh):
    return jax.shard_map(
        per_device,
        mesh=mesh,
        in_specs=(
            P(None, "pix", None),
            P("ch", "pix", None),
            P(None, None, "ch"),
            P("pix", None),
            P("pix", None),
            P("pix", None),
        ),
        out_specs=(P("ch", "pix", None), P(None, None, "ch")),
        check_vma=False,
    )
```

```python
import functools

import jax
import jax.numpy as jnp
from jax import lax
from jax.experimental import pallas as pl
from jax.experimental.pallas import tpu as pltpu
from jax.sharding import PartitionSpec as P

HALO = 4
SIDE = 128
SUB = 16
TILE = 8
INNER = (768, 1280)
OUTER = (1024, 1024)
UNIT = 256
ANY = pl.BlockSpec(memory_space=pl.ANY)
HBM = pl.BlockSpec(memory_space=pltpu.HBM)
VMEM = pl.BlockSpec(memory_space=pltpu.VMEM)
F32, BF16 = jnp.float32, jnp.bfloat16


def params(mib):
    return pltpu.CompilerParams(vmem_limit_bytes=mib * 1024 * 1024)


COST = pl.CostEstimate(flops=1, bytes_accessed=1, transcendentals=0)
LONG = pl.CostEstimate(flops=10**10, bytes_accessed=10**8, transcendentals=0)


def iota(shape, dim):
    return lax.broadcasted_iota(jnp.int32, shape, dim)


def prepare_kernel(
    sides, w_hbm, g_ref, east_ref, south_ref, mask_ref,
    mix_ref, g_out, maps_out, top_ref, bottom_ref, mask_buf, w_ref, sems,
):
    copies = [
        pltpu.make_async_copy(src, dst, sems.at[n])
        for n, (src, dst) in enumerate((
            (w_hbm, w_ref), (mask_ref, mask_buf), (east_ref, maps_out.at[0]),
            (south_ref, maps_out.at[1]), (g_ref, g_out),
        ))
    ]
    for c in copies:
        c.start()
    copies[0].wait()
    nterms, nout, nin = w_ref.shape
    rows, cols = nin * SUB, nout * SUB
    part = nin // sides
    first = (lax.axis_index("ch") + 1) * part
    source = lax.rem(iota((rows, nin), 0) // SUB + first, nin)
    left = (source == iota((rows, nin), 1)).astype(BF16)
    right = (iota((nout, cols), 0) == iota((nout, cols), 1) // SUB).astype(BF16)
    keep = iota((rows, cols), 0) % SUB == iota((rows, cols), 1) % SUB
    for k in range(nterms):
        tall = lax.dot_general(
            left, w_ref[k], (((1,), (1,)), ((), ())), preferred_element_type=F32
        ).astype(BF16)
        full = jnp.dot(tall, right, preferred_element_type=F32)
        mix_ref[:, k * cols : (k + 1) * cols] = jnp.where(keep, full, 0.0).astype(BF16)
    for c in copies[1:4]:
        c.wait()
    mask = mask_buf[...].astype(F32)
    height, total = mask.shape
    east = -2.0 * maps_out[0] * mask * pltpu.roll(mask, total - 1, 1)
    maps_out[0] = jnp.where(iota(mask.shape, 1) == total - 1, 0.0, east)
    maps_out[2] = mask
    copies[4].wait()
    nch = g_out.shape[0]
    for o in range(nch + 3):
        x = g_out[o].astype(F32) if o < nch else maps_out[o - nch]
        top_ref[o] = x[:HALO].astype(BF16)
        bottom_ref[o] = x[height - TILE :][TILE - HALO :].astype(BF16)


def prepare(w, g, east, south, mask, sides):
    nterms, nin, nout = w.shape
    nch, rows, total = g.shape
    edge = jax.ShapeDtypeStruct((nch + 3, HALO, total), BF16)
    args = (w.transpose(0, 2, 1), g, east, south, mask)
    return pl.pallas_call(
        functools.partial(prepare_kernel, sides),
        out_shape=(
            jax.ShapeDtypeStruct((nin * SUB, nterms * nout * SUB), BF16),
            jax.ShapeDtypeStruct(g.shape, g.dtype),
            jax.ShapeDtypeStruct((3, rows, total), F32),
            edge,
            edge,
        ),
        in_specs=[HBM] * 5,
        out_specs=[VMEM] * 5,
        scratch_shapes=[
            pltpu.VMEM((rows, total), jnp.int32),
            pltpu.VMEM((nterms, nout, nin), BF16),
            pltpu.SemaphoreType.DMA((5,)),
        ],
        compiler_params=params(12),
        cost_estimate=COST,
    )(*(pltpu.with_memory_space_constraint(x, pltpu.HBM) for x in args))


def inner_rows(x):
    rows = x.shape[0]
    low = iota((TILE, x.shape[1]), 0) < HALO
    return jnp.concatenate(
        [x[TILE : rows - TILE], jnp.where(low, x[rows - TILE :], x[:TILE])], axis=0
    )


def outer_rows(x, below, above):
    rows = x.shape[0]
    low = iota((TILE, x.shape[1]), 0) < HALO
    return jnp.concatenate(
        [
            x[rows - TILE :], below, above, x[:TILE],
            jnp.where(low, x[TILE : 2 * TILE], x[rows - 2 * TILE : rows - TILE]),
        ],
        axis=0,
    )


def terms_kernel(outer, off, lo, hi, nterms, waits, *refs):
    g_ref, maps_ref, mix_ref = refs[waits : waits + 3]
    below_ref, above_ref = refs[waits + 3 : waits + 5] if outer else (None, None)
    terms_ref, send_ref, w_buf = refs[-3:]
    nch = g_ref.shape[0]
    ext, span = w_buf.shape[1:]
    width = terms_ref.shape[2]
    cols = slice(lo, hi)

    def arrange(x, n):
        x = x.astype(F32)
        if outer:
            below, above = below_ref[n, :, cols], above_ref[n, :, cols]
            return outer_rows(x, below.astype(F32), above.astype(F32))
        return inner_rows(x)

    ew = arrange(maps_ref[0, :, cols], nch)
    south = arrange(maps_ref[1, :, cols], nch + 1)
    mask = arrange(maps_ref[2, :, cols], nch + 2)
    row, col = iota((ext, span), 0), iota((ext, span), 1)
    ww = pltpu.roll(ew, 1, 1)
    if lo == 0:
        ww = jnp.where(col == 0, 0.0, ww)
    sw = -2.0 * south * mask * pltpu.roll(mask, ext - 1, 0)
    for gap in (TILE + HALO - 1, 3 * TILE + HALO - 1) if outer else (ext - HALO - 1,):
        sw = jnp.where(row == gap, 0.0, sw)
    w_buf[0] = ew
    w_buf[1] = ww
    w_buf[2] = sw
    w_buf[3] = pltpu.roll(sw, 1, 0)

    def twice(fields, rounded):
        east, west, south, north = (w_buf[n] for n in range(4))
        out = []
        for v, b in zip(fields, rounded):
            right = pltpu.roll(b, span - 1, 1).astype(F32)
            left = pltpu.roll(b, 1, 1).astype(F32)
            out.append(
                (east * right + west * left)
                + (south * pltpu.roll(v, ext - 1, 0) + north * pltpu.roll(v, 1, 0))
            )
        return out

    def keep(v):
        v = v[:, off : off + width]
        if outer:
            v = jnp.concatenate([v[:TILE], v[2 * TILE : 3 * TILE]], axis=0)
        return v[:SUB].astype(BF16)

    group = 4

    def channels(step, carry):
        chans = [step * group + n for n in range(group)]
        now = [arrange(g_ref[o, :, cols], o) for o in chans]
        prev = None
        for k in range(nterms):
            if k > 0:
                new = twice(now, rounded)
                new = [0.5 * x for x in new] if k == 1 else [x - p for x, p in zip(new, prev)]
                prev, now = now, new
            rounded = [x.astype(BF16) for x in now]
            for o, x in zip(chans, now):
                terms_ref[k * nch + o] = keep(x)
        return carry

    lax.fori_loop(0, nch // group, channels, 0)
    for c in range(0, width, 256):
        x = terms_ref[:, :, c : c + 256].reshape(nterms * nch * SUB, 256)
        y = jnp.dot(mix_ref[: send_ref.shape[0] * SUB], x, preferred_element_type=F32)
        send_ref[:, :, c : c + 256] = y.astype(BF16).reshape(-1, SUB, 256)


def chunk_terms(outer, start, width, g, maps, mix, sent, nterms, beside, waits, cost):
    nch, rows, total = g.shape
    lo, hi = max(0, start - SIDE), min(total, start + width + SIDE)
    ext = 4 * TILE if outer else 3 * TILE
    return pl.pallas_call(
        functools.partial(terms_kernel, outer, start - lo, lo, hi, nterms, len(waits)),
        out_shape=(
            jax.ShapeDtypeStruct((nterms * nch, SUB, width), BF16),
            jax.ShapeDtypeStruct((sent, SUB, width), BF16),
        ),
        in_specs=[ANY] * len(waits) + [VMEM] * (3 + len(beside)),
        out_specs=(VMEM, VMEM),
        scratch_shapes=[pltpu.VMEM((4, ext, hi - lo), F32)],
        compiler_params=params(20),
        cost_estimate=cost,
    )(*waits, g, maps, mix, *beside)


def weights_kernel(places, f_ref, *refs):
    n = len(places)
    terms, (grad_ref, acc) = refs[:n], refs[n:]
    nt = terms[0].shape[0]
    nin, rows, _ = f_ref.shape
    for m, ((outer, start, width), t_ref) in enumerate(zip(places, terms)):
        x = t_ref[...].reshape(nt * SUB, width)
        f = f_ref[:, :, start : start + width].astype(F32)
        if outer:
            f = jnp.concatenate([f[:, rows - TILE :], f[:, :TILE]], axis=1)
        else:
            f = f[:, TILE : rows - TILE]
        f = f.astype(BF16).reshape(nin * SUB, width)
        y = lax.dot_general(x, f, (((1,), (1,)), ((), ())), preferred_element_type=F32)
        if m == 0:
            acc[...] = y
        else:
            acc[...] += y
    r, c = iota((SUB, nin * SUB), 0), iota((SUB, nin * SUB), 1)
    same = (c % SUB == r).astype(F32)
    kept = jnp.sum(acc[...].reshape(nt, SUB, nin * SUB) * same[None], axis=1)
    pick = (iota((nin * SUB, nin), 0) // SUB == iota((nin * SUB, nin), 1)).astype(F32)
    grad_ref[...] = jnp.dot(
        kept, pick, preferred_element_type=F32, precision=lax.Precision.HIGHEST
    )


def weights(places, terms, f):
    nt = terms[0].shape[0]
    nin = f.shape[0]
    return pl.pallas_call(
        functools.partial(weights_kernel, places),
        out_shape=jax.ShapeDtypeStruct((nt, nin), F32),
        in_specs=[VMEM] * (1 + len(terms)),
        out_specs=VMEM,
        scratch_shapes=[pltpu.VMEM((nt * SUB, nin * SUB), F32)],
        compiler_params=params(24),
        cost_estimate=COST,
    )(f, *terms)


def own_kernel(mix_ref, *refs):
    n = len(refs) // 2
    for t_ref, own_ref in zip(refs[:n], refs[n:]):
        kept = own_ref.shape[0]
        for c in range(0, t_ref.shape[2], UNIT):
            x = t_ref[:, :, c : c + UNIT].reshape(-1, UNIT)
            y = jnp.dot(mix_ref[-kept * SUB :], x, preferred_element_type=F32)
            own_ref[:, :, c : c + UNIT] = y.reshape(kept, SUB, UNIT)


def own_parts(mix, terms, kept):
    return pl.pallas_call(
        own_kernel,
        out_shape=[jax.ShapeDtypeStruct((kept, *t.shape[1:]), F32) for t in terms],
        in_specs=[VMEM] * (1 + len(terms)),
        out_specs=[VMEM] * len(terms),
        compiler_params=params(20),
        cost_estimate=COST,
    )(mix, *terms)


def finish_kernel(start, width, from_i, from_o, own_i, got_i, own_o, got_o, *refs):
    out_ref, mark_ref, buf, sems = refs[-4:]
    mark_ref[...] = jnp.zeros_like(mark_ref)
    copies = []
    for n in range(width // UNIT):
        part = slice(n * UNIT, (n + 1) * UNIT)
        i = slice(from_i + n * UNIT, from_i + (n + 1) * UNIT)
        o = slice(from_o + n * UNIT, from_o + (n + 1) * UNIT)
        inner = own_i[:, :, i] + got_i[:, :, i].astype(F32)
        outer = own_o[:, :, o] + got_o[:, :, o].astype(F32)
        rows = jnp.concatenate([outer[:, TILE:], inner, outer[:, :TILE]], axis=1)
        buf[:, :, part] = rows.astype(BF16)
        copies.append(
            pltpu.make_async_copy(
                buf.at[:, :, pl.ds(n * UNIT, UNIT)],
                out_ref.at[:, :, pl.ds(start + n * UNIT, UNIT)],
                sems.at[n],
            )
        )
        copies[-1].start()
    for c in copies:
        c.wait()


def finish(start, width, inner, outer, out, rows, total):
    kept = outer[2].shape[0]
    extra = () if out is None else (out,)
    return pl.pallas_call(
        functools.partial(finish_kernel, start, width, start - inner[0], start - outer[0]),
        out_shape=(
            jax.ShapeDtypeStruct((kept, rows, total), BF16),
            jax.ShapeDtypeStruct((8, 128), F32),
        ),
        in_specs=[VMEM] * 4 + [ANY] * len(extra),
        out_specs=(ANY, VMEM),
        scratch_shapes=[
            pltpu.VMEM((kept, rows, width), BF16),
            pltpu.SemaphoreType.DMA((width // UNIT,)),
        ],
        input_output_aliases={4: 0} if extra else {},
        compiler_params=params(12),
        cost_estimate=COST,
    )(*inner[1:], *outer[1:], *extra)


def add_kernel(count, scale, *refs):
    values = [r[...] for r in refs[:count]]
    while len(values) > 1:
        values = [a + b for a, b in zip(values[::2], values[1::2])]
    refs[-1][...] = values[0] if scale is None else values[0] / jnp.sqrt(F32(scale))


def add(values, waits, scale=None):
    return pl.pallas_call(
        functools.partial(add_kernel, len(values), scale),
        out_shape=jax.ShapeDtypeStruct(values[0].shape, F32),
        in_specs=[VMEM] * len(values) + [ANY] * len(waits),
        out_specs=VMEM,
        compiler_params=params(4),
        cost_estimate=COST,
    )(*values, *waits)


def sum_over_pix(values, size, waits, scale):
    steps, step = [], 1
    while step < size:
        steps.append((step, 4 if step * 2 < size else 2))
        step *= steps[-1][1]
    value = add(values, waits[0])
    for n, (step, count) in enumerate(steps[1:] + steps[:1]):
        last = n + 1 == len(steps)
        moved = [
            lax.ppermute(value, "pix", [(i, i ^ (x * step)) for i in range(size)])
            for x in range(1, count)
        ]
        wait = waits[n + 1] if n + 1 < len(waits) else ()
        value = add([value, *moved], wait, scale if last else None)
    return value


def per_device(features, grad_out, cheb_weight, east_weight, south_weight, pixel_mask):
    nch, rows, total = grad_out.shape
    nterms, nin, _ = cheb_weight.shape
    size, sides = lax.axis_size("pix"), lax.axis_size("ch")
    part = nin // sides
    mix, g, maps, top, bottom = prepare(
        cheb_weight, grad_out, east_weight, south_weight, pixel_mask, sides
    )
    pieces = []

    def chunks(outer, widths, beside, first):
        start = 0
        for width in widths:
            waits = [pieces[-1][1], *first] if pieces else []
            late = outer and start
            waits += [pieces[0][2]] if late else []
            terms, send = chunk_terms(
                outer, start, width, g, maps, mix, part, nterms, beside, waits,
                LONG if late else COST,
            )
            got = lax.ppermute(send, "ch", [(i, i ^ 1) for i in range(sides)])
            pieces.append(((outer, start, width), terms, got))
            start += width
            first = ()

    def local(some):
        places, terms, _ = zip(*some)
        return own_parts(mix, terms, part), weights(places, terms, features)

    n = len(INNER)
    chunks(False, INNER, (), ())
    own_inner, grad_inner = local(pieces)
    down = [(i, i + 1) for i in range(size - 1) if (i + 1) * rows % total]
    up = [(j, i) for i, j in down]
    beside = (lax.ppermute(top, "pix", up), lax.ppermute(bottom, "pix", down))
    chunks(True, OUTER, beside, (own_inner[0], grad_inner))
    own_outer, grad_outer = local(pieces[n:])
    pieces = [
        (place, own, got) for (place, _, got), own in zip(pieces, (*own_inner, *own_outer))
    ]
    out, marks = None, []
    for (_, at, width), outer_own, outer_got in pieces[n:]:
        for (_, first, span), inner_own, inner_got in pieces[:n]:
            lo, hi = max(at, first), min(at + width, first + span)
            if lo < hi:
                inner = (first, inner_own, inner_got)
                outer = (at, outer_own, outer_got)
                out, mark = finish(lo, hi - lo, inner, outer, out, rows, total)
                marks.append(mark)
    waits = ([got for _, _, got in pieces[:n]], own_outer[:1], marks[-2:-1])
    grad = sum_over_pix([grad_inner, grad_outer], size, waits, rows * size * total)
    weight_grad = grad.reshape(nterms, nch, nin).transpose(0, 2, 1)
    return out, weight_grad


def solution(mesh):
    return jax.shard_map(
        per_device,
        mesh=mesh,
        in_specs=(
            P(None, "pix", None),
            P("ch", "pix", None),
            P(None, None, "ch"),
            P("pix", None),
            P("pix", None),
            P("pix", None),
        ),
        out_specs=(P("ch", "pix", None), P(None, None, "ch")),
        check_vma=False,
    )
```

```python
import functools

import jax
import jax.numpy as jnp
from jax import lax
from jax.experimental import pallas as pl
from jax.experimental.pallas import tpu as pltpu
from jax.sharding import PartitionSpec as P

HALO = 4
SIDE = 128
SUB = 16
TILE = 8
INNER = (512, 1536)
OUTER = (1024, 1024)
UNIT = 256
ANY = pl.BlockSpec(memory_space=pl.ANY)
HBM = pl.BlockSpec(memory_space=pltpu.HBM)
VMEM = pl.BlockSpec(memory_space=pltpu.VMEM)
F32, BF16 = jnp.float32, jnp.bfloat16


def params(mib):
    return pltpu.CompilerParams(vmem_limit_bytes=mib * 1024 * 1024)


COST = pl.CostEstimate(flops=1, bytes_accessed=1, transcendentals=0)
LONG = pl.CostEstimate(flops=10**10, bytes_accessed=10**8, transcendentals=0)


def iota(shape, dim):
    return lax.broadcasted_iota(jnp.int32, shape, dim)


def prepare_kernel(
    sides, w_hbm, g_ref, east_ref, south_ref, mask_ref,
    mix_ref, g_out, maps_out, partner_ref, other_ref, mask_buf, w_ref, sems,
):
    copies = [
        pltpu.make_async_copy(src, dst, sems.at[n])
        for n, (src, dst) in enumerate((
            (w_hbm, w_ref), (mask_ref, mask_buf), (east_ref, maps_out.at[0]),
            (south_ref, maps_out.at[1]), (g_ref, g_out),
        ))
    ]
    for c in copies:
        c.start()
    copies[0].wait()
    nterms, nout, nin = w_ref.shape
    rows, cols = nin * SUB, nout * SUB
    part = nin // sides
    first = (lax.axis_index("ch") + 1) * part
    source = lax.rem(iota((rows, nin), 0) // SUB + first, nin)
    left = (source == iota((rows, nin), 1)).astype(BF16)
    right = (iota((nout, cols), 0) == iota((nout, cols), 1) // SUB).astype(BF16)
    keep = iota((rows, cols), 0) % SUB == iota((rows, cols), 1) % SUB
    for k in range(nterms):
        tall = lax.dot_general(
            left, w_ref[k], (((1,), (1,)), ((), ())), preferred_element_type=F32
        ).astype(BF16)
        full = jnp.dot(tall, right, preferred_element_type=F32)
        mix_ref[:, k * cols : (k + 1) * cols] = jnp.where(keep, full, 0.0).astype(BF16)
    for c in copies[1:4]:
        c.wait()
    mask = mask_buf[...].astype(F32)
    height, total = mask.shape
    east = -2.0 * maps_out[0] * mask * pltpu.roll(mask, total - 1, 1)
    maps_out[0] = jnp.where(iota(mask.shape, 1) == total - 1, 0.0, east)
    maps_out[2] = mask
    copies[4].wait()
    nch = g_out.shape[0]
    even = lax.axis_index("pix") % 2 == 0
    for o in range(nch + 3):
        x = g_out[o].astype(F32) if o < nch else maps_out[o - nch]
        top, bottom = x[:HALO].astype(BF16), x[height - TILE :][TILE - HALO :].astype(BF16)
        partner_ref[o] = jnp.where(even, bottom, top)
        other_ref[o] = jnp.where(even, top, bottom)


def prepare(w, g, east, south, mask, sides):
    nterms, nin, nout = w.shape
    nch, rows, total = g.shape
    edge = jax.ShapeDtypeStruct((nch + 3, HALO, total), BF16)
    args = (w.transpose(0, 2, 1), g, east, south, mask)
    return pl.pallas_call(
        functools.partial(prepare_kernel, sides),
        out_shape=(
            jax.ShapeDtypeStruct((nin * SUB, nterms * nout * SUB), BF16),
            jax.ShapeDtypeStruct(g.shape, g.dtype),
            jax.ShapeDtypeStruct((3, rows, total), F32),
            edge,
            edge,
        ),
        in_specs=[HBM] * 5,
        out_specs=[VMEM] * 5,
        scratch_shapes=[
            pltpu.VMEM((rows, total), jnp.int32),
            pltpu.VMEM((nterms, nout, nin), BF16),
            pltpu.SemaphoreType.DMA((5,)),
        ],
        compiler_params=params(12),
        cost_estimate=COST,
    )(*(pltpu.with_memory_space_constraint(x, pltpu.HBM) for x in args))


def inner_rows(x):
    rows = x.shape[0]
    low = iota((TILE, x.shape[1]), 0) < HALO
    return jnp.concatenate(
        [x[TILE : rows - TILE], jnp.where(low, x[rows - TILE :], x[:TILE])], axis=0
    )


def outer_rows(x, below, above):
    rows = x.shape[0]
    low = iota((TILE, x.shape[1]), 0) < HALO
    return jnp.concatenate(
        [
            x[rows - TILE :], below, above, x[:TILE],
            jnp.where(low, x[TILE : 2 * TILE], x[rows - 2 * TILE : rows - TILE]),
        ],
        axis=0,
    )


def terms_kernel(outer, off, lo, hi, nterms, waits, *refs):
    g_ref, maps_ref, mix_ref = refs[waits : waits + 3]
    partner_ref, other_ref = refs[waits + 3 : waits + 5] if outer else (None, None)
    even = lax.axis_index("pix") % 2 == 0
    terms_ref, send_ref, w_buf = refs[-3:]
    nch = g_ref.shape[0]
    ext, span = w_buf.shape[1:]
    width = terms_ref.shape[2]
    cols = slice(lo, hi)

    def arrange(x, n):
        x = x.astype(F32)
        if outer:
            partner = partner_ref[n, :, cols].astype(F32)
            other = other_ref[n, :, cols].astype(F32)
            below, above = jnp.where(even, partner, other), jnp.where(even, other, partner)
            return outer_rows(x, below, above)
        return inner_rows(x)

    ew = arrange(maps_ref[0, :, cols], nch)
    south = arrange(maps_ref[1, :, cols], nch + 1)
    mask = arrange(maps_ref[2, :, cols], nch + 2)
    row, col = iota((ext, span), 0), iota((ext, span), 1)
    ww = pltpu.roll(ew, 1, 1)
    if lo == 0:
        ww = jnp.where(col == 0, 0.0, ww)
    sw = -2.0 * south * mask * pltpu.roll(mask, ext - 1, 0)
    for gap in (TILE + HALO - 1, 3 * TILE + HALO - 1) if outer else (ext - HALO - 1,):
        sw = jnp.where(row == gap, 0.0, sw)
    w_buf[0] = ew
    w_buf[1] = ww
    w_buf[2] = sw
    w_buf[3] = pltpu.roll(sw, 1, 0)

    def twice(fields, rounded):
        east, west, south, north = (w_buf[n] for n in range(4))
        out = []
        for v, b in zip(fields, rounded):
            right = pltpu.roll(b, span - 1, 1).astype(F32)
            left = pltpu.roll(b, 1, 1).astype(F32)
            out.append(
                (east * right + west * left)
                + (south * pltpu.roll(v, ext - 1, 0) + north * pltpu.roll(v, 1, 0))
            )
        return out

    def keep(v):
        v = v[:, off : off + width]
        if outer:
            v = jnp.concatenate([v[:TILE], v[2 * TILE : 3 * TILE]], axis=0)
        return v[:SUB].astype(BF16)

    group = 4

    def channels(step, carry):
        chans = [step * group + n for n in range(group)]
        now = [arrange(g_ref[o, :, cols], o) for o in chans]
        prev = None
        for k in range(nterms):
            if k > 0:
                new = twice(now, rounded)
                new = [0.5 * x for x in new] if k == 1 else [x - p for x, p in zip(new, prev)]
                prev, now = now, new
            rounded = [x.astype(BF16) for x in now]
            for o, x in zip(chans, now):
                terms_ref[k * nch + o] = keep(x)
        return carry

    lax.fori_loop(0, nch // group, channels, 0)
    for c in range(0, width, 256):
        x = terms_ref[:, :, c : c + 256].reshape(nterms * nch * SUB, 256)
        y = jnp.dot(mix_ref[: send_ref.shape[0] * SUB], x, preferred_element_type=F32)
        send_ref[:, :, c : c + 256] = y.astype(BF16).reshape(-1, SUB, 256)


def chunk_terms(outer, start, width, g, maps, mix, sent, nterms, beside, waits, cost):
    nch, rows, total = g.shape
    lo, hi = max(0, start - SIDE), min(total, start + width + SIDE)
    ext = 4 * TILE if outer else 3 * TILE
    return pl.pallas_call(
        functools.partial(terms_kernel, outer, start - lo, lo, hi, nterms, len(waits)),
        out_shape=(
            jax.ShapeDtypeStruct((nterms * nch, SUB, width), BF16),
            jax.ShapeDtypeStruct((sent, SUB, width), BF16),
        ),
        in_specs=[ANY] * len(waits) + [VMEM] * (3 + len(beside)),
        out_specs=(VMEM, VMEM),
        scratch_shapes=[pltpu.VMEM((4, ext, hi - lo), F32)],
        compiler_params=params(20),
        cost_estimate=cost,
    )(*waits, g, maps, mix, *beside)


def weights_kernel(places, f_ref, *refs):
    n = len(places)
    terms, (grad_ref, acc) = refs[:n], refs[n:]
    nt = terms[0].shape[0]
    nin, rows, _ = f_ref.shape
    for m, ((outer, start, width), t_ref) in enumerate(zip(places, terms)):
        x = t_ref[...].reshape(nt * SUB, width)
        f = f_ref[:, :, start : start + width].astype(F32)
        if outer:
            f = jnp.concatenate([f[:, rows - TILE :], f[:, :TILE]], axis=1)
        else:
            f = f[:, TILE : rows - TILE]
        f = f.astype(BF16).reshape(nin * SUB, width)
        y = lax.dot_general(x, f, (((1,), (1,)), ((), ())), preferred_element_type=F32)
        if m == 0:
            acc[...] = y
        else:
            acc[...] += y
    r, c = iota((SUB, nin * SUB), 0), iota((SUB, nin * SUB), 1)
    same = (c % SUB == r).astype(F32)
    kept = jnp.sum(acc[...].reshape(nt, SUB, nin * SUB) * same[None], axis=1)
    pick = (iota((nin * SUB, nin), 0) // SUB == iota((nin * SUB, nin), 1)).astype(F32)
    grad_ref[...] = jnp.dot(
        kept, pick, preferred_element_type=F32, precision=lax.Precision.HIGHEST
    )


def weights(places, terms, f):
    nt = terms[0].shape[0]
    nin = f.shape[0]
    return pl.pallas_call(
        functools.partial(weights_kernel, places),
        out_shape=jax.ShapeDtypeStruct((nt, nin), F32),
        in_specs=[VMEM] * (1 + len(terms)),
        out_specs=VMEM,
        scratch_shapes=[pltpu.VMEM((nt * SUB, nin * SUB), F32)],
        compiler_params=params(24),
        cost_estimate=COST,
    )(f, *terms)


def own_kernel(mix_ref, *refs):
    n = len(refs) // 2
    for t_ref, own_ref in zip(refs[:n], refs[n:]):
        kept = own_ref.shape[0]
        for c in range(0, t_ref.shape[2], UNIT):
            x = t_ref[:, :, c : c + UNIT].reshape(-1, UNIT)
            y = jnp.dot(mix_ref[-kept * SUB :], x, preferred_element_type=F32)
            own_ref[:, :, c : c + UNIT] = y.reshape(kept, SUB, UNIT)


def own_parts(mix, terms, kept):
    return pl.pallas_call(
        own_kernel,
        out_shape=[jax.ShapeDtypeStruct((kept, *t.shape[1:]), F32) for t in terms],
        in_specs=[VMEM] * (1 + len(terms)),
        out_specs=[VMEM] * len(terms),
        compiler_params=params(20),
        cost_estimate=COST,
    )(mix, *terms)


def finish_kernel(start, width, from_i, from_o, own_i, got_i, own_o, got_o, *refs):
    out_ref, mark_ref, buf, sems = refs[-4:]
    mark_ref[...] = jnp.zeros_like(mark_ref)
    copies = []
    for n in range(width // UNIT):
        part = slice(n * UNIT, (n + 1) * UNIT)
        i = slice(from_i + n * UNIT, from_i + (n + 1) * UNIT)
        o = slice(from_o + n * UNIT, from_o + (n + 1) * UNIT)
        inner = own_i[:, :, i] + got_i[:, :, i].astype(F32)
        outer = own_o[:, :, o] + got_o[:, :, o].astype(F32)
        rows = jnp.concatenate([outer[:, TILE:], inner, outer[:, :TILE]], axis=1)
        buf[:, :, part] = rows.astype(BF16)
        copies.append(
            pltpu.make_async_copy(
                buf.at[:, :, pl.ds(n * UNIT, UNIT)],
                out_ref.at[:, :, pl.ds(start + n * UNIT, UNIT)],
                sems.at[n],
            )
        )
        copies[-1].start()
    for c in copies:
        c.wait()


def finish(start, width, inner, outer, out, rows, total):
    kept = outer[2].shape[0]
    extra = () if out is None else (out,)
    return pl.pallas_call(
        functools.partial(finish_kernel, start, width, start - inner[0], start - outer[0]),
        out_shape=(
            jax.ShapeDtypeStruct((kept, rows, total), BF16),
            jax.ShapeDtypeStruct((8, 128), F32),
        ),
        in_specs=[VMEM] * 4 + [ANY] * len(extra),
        out_specs=(ANY, VMEM),
        scratch_shapes=[
            pltpu.VMEM((kept, rows, width), BF16),
            pltpu.SemaphoreType.DMA((width // UNIT,)),
        ],
        input_output_aliases={4: 0} if extra else {},
        compiler_params=params(12),
        cost_estimate=COST,
    )(*inner[1:], *outer[1:], *extra)


def add_kernel(count, scale, *refs):
    values = [r[...] for r in refs[:count]]
    while len(values) > 1:
        values = [a + b for a, b in zip(values[::2], values[1::2])]
    refs[-1][...] = values[0] if scale is None else values[0] / jnp.sqrt(F32(scale))


def add(values, waits, scale=None):
    return pl.pallas_call(
        functools.partial(add_kernel, len(values), scale),
        out_shape=jax.ShapeDtypeStruct(values[0].shape, F32),
        in_specs=[VMEM] * len(values) + [ANY] * len(waits),
        out_specs=VMEM,
        compiler_params=params(4),
        cost_estimate=COST,
    )(*values, *waits)


def sum_over_pix(values, size, waits, scale):
    steps, step = [], 1
    while step < size:
        steps.append((step, 4 if step * 2 < size else 2))
        step *= steps[-1][1]
    value = add(values, waits[0])
    for n, (step, count) in enumerate(steps[1:] + steps[:1]):
        last = n + 1 == len(steps)
        moved = [
            lax.ppermute(value, "pix", [(i, i ^ (x * step)) for i in range(size)])
            for x in range(1, count)
        ]
        wait = waits[n + 1] if n + 1 < len(waits) else ()
        value = add([value, *moved], wait, scale if last else None)
    return value


def per_device(features, grad_out, cheb_weight, east_weight, south_weight, pixel_mask):
    nch, rows, total = grad_out.shape
    nterms, nin, _ = cheb_weight.shape
    size, sides = lax.axis_size("pix"), lax.axis_size("ch")
    part = nin // sides
    mix, g, maps, to_partner, to_other = prepare(
        cheb_weight, grad_out, east_weight, south_weight, pixel_mask, sides
    )
    pieces = []

    def chunks(outer, widths, beside, first):
        start = 0
        for width in widths:
            waits = [pieces[-1][1], *first] if pieces else []
            late = outer and start
            waits += [pieces[0][2]] if late else []
            terms, send = chunk_terms(
                outer, start, width, g, maps, mix, part, nterms, beside, waits,
                LONG if late else COST,
            )
            got = lax.ppermute(send, "ch", [(i, i ^ 1) for i in range(sides)])
            pieces.append(((outer, start, width), terms, got))
            start += width
            first = ()

    def local(some):
        places, terms, _ = zip(*some)
        return own_parts(mix, terms, part), weights(places, terms, features)

    n = len(INNER)
    chunks(False, INNER, (), ())
    own_inner, grad_inner = local(pieces)
    def swap(x, first):
        pairs = [(i, i + 1) for i in range(first, size - 1, 2) if (i + 1) * rows % total]
        return lax.ppermute(x, "pix", pairs + [(j, i) for i, j in pairs])

    beside = (swap(to_partner, 0), swap(to_other, 1))
    chunks(True, OUTER, beside, (own_inner[0], grad_inner))
    own_outer, grad_outer = local(pieces[n:])
    pieces = [
        (place, own, got) for (place, _, got), own in zip(pieces, (*own_inner, *own_outer))
    ]
    out, marks = None, []
    for (_, at, width), outer_own, outer_got in pieces[n:]:
        for (_, first, span), inner_own, inner_got in pieces[:n]:
            lo, hi = max(at, first), min(at + width, first + span)
            if lo < hi:
                inner = (first, inner_own, inner_got)
                outer = (at, outer_own, outer_got)
                out, mark = finish(lo, hi - lo, inner, outer, out, rows, total)
                marks.append(mark)
    waits = ([got for _, _, got in pieces[:n]], own_outer[:1], marks[-2:-1], marks[-1:])
    grad = sum_over_pix([grad_inner, grad_outer], size, waits, rows * size * total)
    weight_grad = grad.reshape(nterms, nch, nin).transpose(0, 2, 1)
    return out, weight_grad


def solution(mesh):
    return jax.shard_map(
        per_device,
        mesh=mesh,
        in_specs=(
            P(None, "pix", None),
            P("ch", "pix", None),
            P(None, None, "ch"),
            P("pix", None),
            P("pix", None),
            P("pix", None),
        ),
        out_specs=(P("ch", "pix", None), P(None, None, "ch")),
        check_vma=False,
    )
```

```python
import functools

import jax
import jax.numpy as jnp
from jax import lax
from jax.experimental import pallas as pl
from jax.experimental.pallas import tpu as pltpu
from jax.sharding import PartitionSpec as P

HALO = 4
SIDE = 128
SUB = 16
TILE = 8
INNER = (512, 1536)
OUTER = (1024, 1024)
UNIT = 256
NEED = 3
ANY = pl.BlockSpec(memory_space=pl.ANY)
HBM = pl.BlockSpec(memory_space=pltpu.HBM)
VMEM = pl.BlockSpec(memory_space=pltpu.VMEM)
F32, BF16 = jnp.float32, jnp.bfloat16


def params(mib):
    return pltpu.CompilerParams(vmem_limit_bytes=mib * 1024 * 1024)


COST = pl.CostEstimate(flops=1, bytes_accessed=1, transcendentals=0)
LONG = pl.CostEstimate(flops=10**10, bytes_accessed=10**8, transcendentals=0)


def iota(shape, dim):
    return lax.broadcasted_iota(jnp.int32, shape, dim)


def dense_rows(n, nch):
    if n < nch:
        return n * NEED, NEED
    before = nch * NEED
    return (before, NEED - 1) if n == nch else (before + (n - nch) * NEED - 1, NEED)


def prepare_kernel(
    sides, w_hbm, g_ref, east_ref, south_ref, mask_ref,
    mix_ref, g_out, maps_out, partner_ref, other_ref, mask_buf, w_ref, dense, sems,
):
    copies = [
        pltpu.make_async_copy(src, dst, sems.at[n])
        for n, (src, dst) in enumerate((
            (w_hbm, w_ref), (mask_ref, mask_buf), (east_ref, maps_out.at[0]),
            (south_ref, maps_out.at[1]), (g_ref, g_out),
        ))
    ]
    for c in copies:
        c.start()
    copies[0].wait()
    nterms, nout, nin = w_ref.shape
    rows, cols = nin * SUB, nout * SUB
    part = nin // sides
    first = (lax.axis_index("ch") + 1) * part
    source = lax.rem(iota((rows, nin), 0) // SUB + first, nin)
    left = (source == iota((rows, nin), 1)).astype(BF16)
    right = (iota((nout, cols), 0) == iota((nout, cols), 1) // SUB).astype(BF16)
    keep = iota((rows, cols), 0) % SUB == iota((rows, cols), 1) % SUB
    for k in range(nterms):
        tall = lax.dot_general(
            left, w_ref[k], (((1,), (1,)), ((), ())), preferred_element_type=F32
        ).astype(BF16)
        full = jnp.dot(tall, right, preferred_element_type=F32)
        mix_ref[:, k * cols : (k + 1) * cols] = jnp.where(keep, full, 0.0).astype(BF16)
    for c in copies[1:4]:
        c.wait()
    mask = mask_buf[...].astype(F32)
    height, total = mask.shape
    east = -2.0 * maps_out[0] * mask * pltpu.roll(mask, total - 1, 1)
    maps_out[0] = jnp.where(iota(mask.shape, 1) == total - 1, 0.0, east)
    maps_out[2] = mask
    copies[4].wait()
    nch = g_out.shape[0]
    even = lax.axis_index("pix") % 2 == 0
    for o in range(nch + 3):
        x = g_out[o].astype(F32) if o < nch else maps_out[o - nch]
        head, tail = x[:TILE], x[height - TILE :]
        partner = jnp.where(even, tail[TILE - HALO :], head[:HALO])
        partner_ref[o] = partner.astype(BF16)
        at, count = dense_rows(o, nch)
        other = jnp.where(even, head, pltpu.roll(tail, count, 0))
        dense[at : at + count] = other[:count]
    other_ref[...] = dense[...].astype(BF16)


def prepare(w, g, east, south, mask, sides):
    nterms, nin, nout = w.shape
    nch, rows, total = g.shape
    dense = (nch + 3) * NEED - 1
    args = (w.transpose(0, 2, 1), g, east, south, mask)
    return pl.pallas_call(
        functools.partial(prepare_kernel, sides),
        out_shape=(
            jax.ShapeDtypeStruct((nin * SUB, nterms * nout * SUB), BF16),
            jax.ShapeDtypeStruct(g.shape, g.dtype),
            jax.ShapeDtypeStruct((3, rows, total), F32),
            jax.ShapeDtypeStruct((nch + 3, HALO, total), BF16),
            jax.ShapeDtypeStruct((dense, total), BF16),
        ),
        in_specs=[HBM] * 5,
        out_specs=[VMEM] * 5,
        scratch_shapes=[
            pltpu.VMEM((rows, total), jnp.int32),
            pltpu.VMEM((nterms, nout, nin), BF16),
            pltpu.VMEM((dense, total), F32),
            pltpu.SemaphoreType.DMA((5,)),
        ],
        compiler_params=params(12),
        cost_estimate=COST,
    )(*(pltpu.with_memory_space_constraint(x, pltpu.HBM) for x in args))


def inner_rows(x):
    rows = x.shape[0]
    low = iota((TILE, x.shape[1]), 0) < HALO
    return jnp.concatenate(
        [x[TILE : rows - TILE], jnp.where(low, x[rows - TILE :], x[:TILE])], axis=0
    )


def outer_rows(x, beside):
    rows = x.shape[0]
    low = iota((TILE, x.shape[1]), 0) < HALO
    return jnp.concatenate(
        [
            x[rows - TILE :], beside, x[:TILE],
            jnp.where(low, x[TILE : 2 * TILE], x[rows - 2 * TILE : rows - TILE]),
        ],
        axis=0,
    )


def terms_kernel(outer, off, lo, hi, nterms, waits, *refs):
    g_ref, maps_ref, mix_ref = refs[waits : waits + 3]
    partner_ref, other_ref = refs[waits + 3 : waits + 5] if outer else (None, None)
    (terms_ref, send_ref, w_buf), tiles = refs[-5:-2] if outer else refs[-3:], refs[-1]
    nch = g_ref.shape[0]
    ext, span = w_buf.shape[1:]
    width = terms_ref.shape[2]
    cols = slice(lo, hi)
    if outer:
        below = 1 - lax.axis_index("pix") % 2
        side = (iota((TILE, span), 0) < HALO).astype(jnp.int32)
        dense = refs[-2]
        count = dense.shape[0] - 2 * TILE
        dense[:TILE] = jnp.zeros((TILE, span), F32)
        dense[TILE : TILE + count] = other_ref[:, cols].astype(F32)
        dense[TILE + count :] = jnp.zeros((TILE, span), F32)
        for n in range(nch + 3):
            at, many = dense_rows(n, nch)
            last, first = dense[at + many : at + many + TILE], dense[TILE + at : 2 * TILE + at]
            tiles[n] = jnp.where(below == 1, last, first)

    def arrange(x, n):
        x = x.astype(F32)
        if outer:
            partner = partner_ref[n, :, cols].astype(F32)
            partner = jnp.concatenate([partner, partner], axis=0)
            return outer_rows(x, jnp.where(side == below, partner, tiles[n]))
        return inner_rows(x)

    ew = arrange(maps_ref[0, :, cols], nch)
    south = arrange(maps_ref[1, :, cols], nch + 1)
    mask = arrange(maps_ref[2, :, cols], nch + 2)
    row, col = iota((ext, span), 0), iota((ext, span), 1)
    ww = pltpu.roll(ew, 1, 1)
    if lo == 0:
        ww = jnp.where(col == 0, 0.0, ww)
    sw = -2.0 * south * mask * pltpu.roll(mask, ext - 1, 0)
    for gap in (TILE + HALO - 1, 3 * TILE + HALO - 1) if outer else (ext - HALO - 1,):
        sw = jnp.where(row == gap, 0.0, sw)
    w_buf[0] = ew
    w_buf[1] = ww
    w_buf[2] = sw
    w_buf[3] = pltpu.roll(sw, 1, 0)

    def twice(fields, rounded):
        east, west, south, north = (w_buf[n] for n in range(4))
        out = []
        for v, b in zip(fields, rounded):
            right = pltpu.roll(b, span - 1, 1).astype(F32)
            left = pltpu.roll(b, 1, 1).astype(F32)
            out.append(
                (east * right + west * left)
                + (south * pltpu.roll(v, ext - 1, 0) + north * pltpu.roll(v, 1, 0))
            )
        return out

    def keep(v):
        v = v[:, off : off + width]
        if outer:
            v = jnp.concatenate([v[:TILE], v[2 * TILE : 3 * TILE]], axis=0)
        return v[:SUB].astype(BF16)

    group = 4

    def channels(step, carry):
        chans = [step * group + n for n in range(group)]
        now = [arrange(g_ref[o, :, cols], o) for o in chans]
        prev = None
        for k in range(nterms):
            if k > 0:
                new = twice(now, rounded)
                new = [0.5 * x for x in new] if k == 1 else [x - p for x, p in zip(new, prev)]
                prev, now = now, new
            rounded = [x.astype(BF16) for x in now]
            for o, x in zip(chans, now):
                terms_ref[k * nch + o] = keep(x)
        return carry

    lax.fori_loop(0, nch // group, channels, 0)
    for c in range(0, width, 256):
        x = terms_ref[:, :, c : c + 256].reshape(nterms * nch * SUB, 256)
        y = jnp.dot(mix_ref[: send_ref.shape[0] * SUB], x, preferred_element_type=F32)
        send_ref[:, :, c : c + 256] = y.astype(BF16).reshape(-1, SUB, 256)


def chunk_terms(outer, start, width, g, maps, mix, sent, nterms, beside, waits, cost):
    nch, rows, total = g.shape
    lo, hi = max(0, start - SIDE), min(total, start + width + SIDE)
    ext = 4 * TILE if outer else 3 * TILE
    halo = []
    if outer:
        halo = [
            pltpu.VMEM((beside[1].shape[0] + 2 * TILE, hi - lo), F32),
            pltpu.VMEM((nch + 3, TILE, hi - lo), F32),
        ]
    return pl.pallas_call(
        functools.partial(terms_kernel, outer, start - lo, lo, hi, nterms, len(waits)),
        out_shape=(
            jax.ShapeDtypeStruct((nterms * nch, SUB, width), BF16),
            jax.ShapeDtypeStruct((sent, SUB, width), BF16),
        ),
        in_specs=[ANY] * len(waits) + [VMEM] * (3 + len(beside)),
        out_specs=(VMEM, VMEM),
        scratch_shapes=[pltpu.VMEM((4, ext, hi - lo), F32)] + halo,
        compiler_params=params(20),
        cost_estimate=cost,
    )(*waits, g, maps, mix, *beside)


def weights_kernel(places, f_ref, *refs):
    n = len(places)
    terms, (grad_ref, acc) = refs[:n], refs[n:]
    nt = terms[0].shape[0]
    nin, rows, _ = f_ref.shape
    for m, ((outer, start, width), t_ref) in enumerate(zip(places, terms)):
        x = t_ref[...].reshape(nt * SUB, width)
        f = f_ref[:, :, start : start + width].astype(F32)
        if outer:
            f = jnp.concatenate([f[:, rows - TILE :], f[:, :TILE]], axis=1)
        else:
            f = f[:, TILE : rows - TILE]
        f = f.astype(BF16).reshape(nin * SUB, width)
        y = lax.dot_general(x, f, (((1,), (1,)), ((), ())), preferred_element_type=F32)
        if m == 0:
            acc[...] = y
        else:
            acc[...] += y
    r, c = iota((SUB, nin * SUB), 0), iota((SUB, nin * SUB), 1)
    same = (c % SUB == r).astype(F32)
    kept = jnp.sum(acc[...].reshape(nt, SUB, nin * SUB) * same[None], axis=1)
    pick = (iota((nin * SUB, nin), 0) // SUB == iota((nin * SUB, nin), 1)).astype(F32)
    grad_ref[...] = jnp.dot(
        kept, pick, preferred_element_type=F32, precision=lax.Precision.HIGHEST
    )


def weights(places, terms, f):
    nt = terms[0].shape[0]
    nin = f.shape[0]
    return pl.pallas_call(
        functools.partial(weights_kernel, places),
        out_shape=jax.ShapeDtypeStruct((nt, nin), F32),
        in_specs=[VMEM] * (1 + len(terms)),
        out_specs=VMEM,
        scratch_shapes=[pltpu.VMEM((nt * SUB, nin * SUB), F32)],
        compiler_params=params(24),
        cost_estimate=COST,
    )(f, *terms)


def own_kernel(mix_ref, *refs):
    n = len(refs) // 2
    for t_ref, own_ref in zip(refs[:n], refs[n:]):
        kept = own_ref.shape[0]
        for c in range(0, t_ref.shape[2], UNIT):
            x = t_ref[:, :, c : c + UNIT].reshape(-1, UNIT)
            y = jnp.dot(mix_ref[-kept * SUB :], x, preferred_element_type=F32)
            own_ref[:, :, c : c + UNIT] = y.reshape(kept, SUB, UNIT)


def own_parts(mix, terms, kept):
    return pl.pallas_call(
        own_kernel,
        out_shape=[jax.ShapeDtypeStruct((kept, *t.shape[1:]), F32) for t in terms],
        in_specs=[VMEM] * (1 + len(terms)),
        out_specs=[VMEM] * len(terms),
        compiler_params=params(20),
        cost_estimate=COST,
    )(mix, *terms)


def finish_kernel(start, width, from_i, from_o, own_i, got_i, own_o, got_o, *refs):
    out_ref, mark_ref, buf, sems = refs[-4:]
    mark_ref[...] = jnp.zeros_like(mark_ref)
    copies = []
    for n in range(width // UNIT):
        part = slice(n * UNIT, (n + 1) * UNIT)
        i = slice(from_i + n * UNIT, from_i + (n + 1) * UNIT)
        o = slice(from_o + n * UNIT, from_o + (n + 1) * UNIT)
        inner = own_i[:, :, i] + got_i[:, :, i].astype(F32)
        outer = own_o[:, :, o] + got_o[:, :, o].astype(F32)
        rows = jnp.concatenate([outer[:, TILE:], inner, outer[:, :TILE]], axis=1)
        buf[:, :, part] = rows.astype(BF16)
        copies.append(
            pltpu.make_async_copy(
                buf.at[:, :, pl.ds(n * UNIT, UNIT)],
                out_ref.at[:, :, pl.ds(start + n * UNIT, UNIT)],
                sems.at[n],
            )
        )
        copies[-1].start()
    for c in copies:
        c.wait()


def finish(start, width, inner, outer, out, rows, total):
    kept = outer[2].shape[0]
    extra = () if out is None else (out,)
    return pl.pallas_call(
        functools.partial(finish_kernel, start, width, start - inner[0], start - outer[0]),
        out_shape=(
            jax.ShapeDtypeStruct((kept, rows, total), BF16),
            jax.ShapeDtypeStruct((8, 128), F32),
        ),
        in_specs=[VMEM] * 4 + [ANY] * len(extra),
        out_specs=(ANY, VMEM),
        scratch_shapes=[
            pltpu.VMEM((kept, rows, width), BF16),
            pltpu.SemaphoreType.DMA((width // UNIT,)),
        ],
        input_output_aliases={4: 0} if extra else {},
        compiler_params=params(12),
        cost_estimate=COST,
    )(*inner[1:], *outer[1:], *extra)


def add_kernel(count, scale, *refs):
    values = [r[...] for r in refs[:count]]
    while len(values) > 1:
        values = [a + b for a, b in zip(values[::2], values[1::2])]
    refs[-1][...] = values[0] if scale is None else values[0] / jnp.sqrt(F32(scale))


def add(values, waits, scale=None):
    return pl.pallas_call(
        functools.partial(add_kernel, len(values), scale),
        out_shape=jax.ShapeDtypeStruct(values[0].shape, F32),
        in_specs=[VMEM] * len(values) + [ANY] * len(waits),
        out_specs=VMEM,
        compiler_params=params(4),
        cost_estimate=COST,
    )(*values, *waits)


def sum_over_pix(values, size, waits, scale):
    steps, step = [], 1
    while step < size:
        steps.append((step, 4 if step * 2 < size else 2))
        step *= steps[-1][1]
    value = add(values, waits[0])
    for n, (step, count) in enumerate(steps[1:] + steps[:1]):
        last = n + 1 == len(steps)
        moved = [
            lax.ppermute(value, "pix", [(i, i ^ (x * step)) for i in range(size)])
            for x in range(1, count)
        ]
        wait = waits[n + 1] if n + 1 < len(waits) else ()
        value = add([value, *moved], wait, scale if last else None)
    return value


def per_device(features, grad_out, cheb_weight, east_weight, south_weight, pixel_mask):
    nch, rows, total = grad_out.shape
    nterms, nin, _ = cheb_weight.shape
    size, sides = lax.axis_size("pix"), lax.axis_size("ch")
    part = nin // sides
    mix, g, maps, to_partner, to_other = prepare(
        cheb_weight, grad_out, east_weight, south_weight, pixel_mask, sides
    )
    pieces = []

    def chunks(outer, widths, beside, first):
        start = 0
        for width in widths:
            waits = [pieces[-1][1], *first] if pieces else []
            late = outer and start
            waits += [pieces[0][2]] if late else []
            terms, send = chunk_terms(
                outer, start, width, g, maps, mix, part, nterms, beside, waits,
                LONG if late else COST,
            )
            got = lax.ppermute(send, "ch", [(i, i ^ 1) for i in range(sides)])
            pieces.append(((outer, start, width), terms, got))
            start += width
            first = ()

    def local(some):
        places, terms, _ = zip(*some)
        return own_parts(mix, terms, part), weights(places, terms, features)

    n = len(INNER)
    chunks(False, INNER, (), ())
    own_inner, grad_inner = local(pieces)
    def swap(x, first):
        pairs = [(i, i + 1) for i in range(first, size - 1, 2) if (i + 1) * rows % total]
        return lax.ppermute(x, "pix", pairs + [(j, i) for i, j in pairs])

    beside = (swap(to_partner, 0), swap(to_other, 1))
    chunks(True, OUTER, beside, (own_inner[0], grad_inner))
    own_outer, grad_outer = local(pieces[n:])
    pieces = [
        (place, own, got) for (place, _, got), own in zip(pieces, (*own_inner, *own_outer))
    ]
    out, marks = None, []
    for (_, at, width), outer_own, outer_got in pieces[n:]:
        for (_, first, span), inner_own, inner_got in pieces[:n]:
            lo, hi = max(at, first), min(at + width, first + span)
            if lo < hi:
                inner = (first, inner_own, inner_got)
                outer = (at, outer_own, outer_got)
                out, mark = finish(lo, hi - lo, inner, outer, out, rows, total)
                marks.append(mark)
    waits = ([got for _, _, got in pieces[:n]], own_outer[:1], marks[-2:-1], marks[-1:])
    grad = sum_over_pix([grad_inner, grad_outer], size, waits, rows * size * total)
    weight_grad = grad.reshape(nterms, nch, nin).transpose(0, 2, 1)
    return out, weight_grad


def solution(mesh):
    return jax.shard_map(
        per_device,
        mesh=mesh,
        in_specs=(
            P(None, "pix", None),
            P("ch", "pix", None),
            P(None, None, "ch"),
            P("pix", None),
            P("pix", None),
            P("pix", None),
        ),
        out_specs=(P("ch", "pix", None), P(None, None, "ch")),
        check_vma=False,
    )
```

```python
import functools

import jax
import jax.numpy as jnp
from jax import lax
from jax.experimental import pallas as pl
from jax.experimental.pallas import tpu as pltpu
from jax.sharding import PartitionSpec as P

HALO = 4
SIDE = 128
SUB = 16
TILE = 8
INNER = (512, 1536)
OUTER = (1024, 1024)
UNIT = 256
PARTS = 4
NEED = 3
ANY = pl.BlockSpec(memory_space=pl.ANY)
HBM = pl.BlockSpec(memory_space=pltpu.HBM)
VMEM = pl.BlockSpec(memory_space=pltpu.VMEM)
F32, BF16 = jnp.float32, jnp.bfloat16


def params(mib):
    return pltpu.CompilerParams(vmem_limit_bytes=mib * 1024 * 1024)


COST = pl.CostEstimate(flops=1, bytes_accessed=1, transcendentals=0)
LONG = pl.CostEstimate(flops=10**10, bytes_accessed=10**8, transcendentals=0)


def iota(shape, dim):
    return lax.broadcasted_iota(jnp.int32, shape, dim)


def dense_rows(n, nch):
    if n < nch:
        return n * NEED, NEED
    before = nch * NEED
    return (before, NEED - 1) if n == nch else (before + (n - nch) * NEED - 1, NEED)


def prepare_kernel(
    sides, w_hbm, g_ref, east_ref, south_ref, mask_ref,
    mix_ref, g_out, maps_out, partner_ref, other_ref, mask_buf, w_ref, dense, sems,
):
    nch = g_out.shape[0]
    some = nch // PARTS
    pairs = [
        (w_hbm, w_ref), (mask_ref, mask_buf), (east_ref, maps_out.at[0]), (south_ref, maps_out.at[1]),
    ]
    for n in range(PARTS):
        part = pl.ds(n * some, some)
        pairs.append((g_ref.at[part], g_out.at[part]))
    copies = [
        pltpu.make_async_copy(src, dst, sems.at[n]) for n, (src, dst) in enumerate(pairs)
    ]
    for c in copies:
        c.start()
    copies[0].wait()
    nterms, nout, nin = w_ref.shape
    rows, cols = nin * SUB, nout * SUB
    part = nin // sides
    first = (lax.axis_index("ch") + 1) * part
    source = lax.rem(iota((rows, nin), 0) // SUB + first, nin)
    left = (source == iota((rows, nin), 1)).astype(BF16)
    right = (iota((nout, cols), 0) == iota((nout, cols), 1) // SUB).astype(BF16)
    keep = iota((rows, cols), 0) % SUB == iota((rows, cols), 1) % SUB
    for k in range(nterms):
        tall = lax.dot_general(
            left, w_ref[k], (((1,), (1,)), ((), ())), preferred_element_type=F32
        ).astype(BF16)
        full = jnp.dot(tall, right, preferred_element_type=F32)
        mix_ref[:, k * cols : (k + 1) * cols] = jnp.where(keep, full, 0.0).astype(BF16)
    for c in copies[1:4]:
        c.wait()
    mask = mask_buf[...].astype(F32)
    height, total = mask.shape
    east = -2.0 * maps_out[0] * mask * pltpu.roll(mask, total - 1, 1)
    maps_out[0] = jnp.where(iota(mask.shape, 1) == total - 1, 0.0, east)
    maps_out[2] = mask
    even = lax.axis_index("pix") % 2 == 0
    for o in range(nch + 3):
        if o < nch and o % some == 0:
            copies[4 + o // some].wait()
        x = g_out[o].astype(F32) if o < nch else maps_out[o - nch]
        head, tail = x[:TILE], x[height - TILE :]
        partner = jnp.where(even, tail[TILE - HALO :], head[:HALO])
        partner_ref[o] = partner.astype(BF16)
        at, count = dense_rows(o, nch)
        other = jnp.where(even, head, pltpu.roll(tail, count, 0))
        dense[at : at + count] = other[:count]
    other_ref[...] = dense[...].astype(BF16)


def prepare(w, g, east, south, mask, sides):
    nterms, nin, nout = w.shape
    nch, rows, total = g.shape
    dense = (nch + 3) * NEED - 1
    args = (w.transpose(0, 2, 1), g, east, south, mask)
    return pl.pallas_call(
        functools.partial(prepare_kernel, sides),
        out_shape=(
            jax.ShapeDtypeStruct((nin * SUB, nterms * nout * SUB), BF16),
            jax.ShapeDtypeStruct(g.shape, g.dtype),
            jax.ShapeDtypeStruct((3, rows, total), F32),
            jax.ShapeDtypeStruct((nch + 3, HALO, total), BF16),
            jax.ShapeDtypeStruct((dense, total), BF16),
        ),
        in_specs=[HBM] * 5,
        out_specs=[VMEM] * 5,
        scratch_shapes=[
            pltpu.VMEM((rows, total), jnp.int32),
            pltpu.VMEM((nterms, nout, nin), BF16),
            pltpu.VMEM((dense, total), F32),
            pltpu.SemaphoreType.DMA((4 + PARTS,)),
        ],
        compiler_params=params(12),
        cost_estimate=COST,
    )(*(pltpu.with_memory_space_constraint(x, pltpu.HBM) for x in args))


def inner_rows(x):
    rows = x.shape[0]
    low = iota((TILE, x.shape[1]), 0) < HALO
    return jnp.concatenate(
        [x[TILE : rows - TILE], jnp.where(low, x[rows - TILE :], x[:TILE])], axis=0
    )


def outer_rows(x, beside):
    rows = x.shape[0]
    low = iota((TILE, x.shape[1]), 0) < HALO
    return jnp.concatenate(
        [
            x[rows - TILE :], beside, x[:TILE],
            jnp.where(low, x[TILE : 2 * TILE], x[rows - 2 * TILE : rows - TILE]),
        ],
        axis=0,
    )


def terms_kernel(outer, off, lo, hi, nterms, waits, *refs):
    g_ref, maps_ref, mix_ref = refs[waits : waits + 3]
    partner_ref, other_ref = refs[waits + 3 : waits + 5] if outer else (None, None)
    (terms_ref, send_ref, w_buf), tiles = refs[-5:-2] if outer else refs[-3:], refs[-1]
    nch = g_ref.shape[0]
    ext, span = w_buf.shape[1:]
    width = terms_ref.shape[2]
    cols = slice(lo, hi)
    if outer:
        below = 1 - lax.axis_index("pix") % 2
        side = (iota((TILE, span), 0) < HALO).astype(jnp.int32)
        dense = refs[-2]
        count = dense.shape[0] - 2 * TILE
        dense[:TILE] = jnp.zeros((TILE, span), F32)
        dense[TILE : TILE + count] = other_ref[:, cols].astype(F32)
        dense[TILE + count :] = jnp.zeros((TILE, span), F32)
        for n in range(nch + 3):
            at, many = dense_rows(n, nch)
            last, first = dense[at + many : at + many + TILE], dense[TILE + at : 2 * TILE + at]
            tiles[n] = jnp.where(below == 1, last, first)

    def arrange(x, n):
        x = x.astype(F32)
        if outer:
            partner = partner_ref[n, :, cols].astype(F32)
            partner = jnp.concatenate([partner, partner], axis=0)
            return outer_rows(x, jnp.where(side == below, partner, tiles[n]))
        return inner_rows(x)

    ew = arrange(maps_ref[0, :, cols], nch)
    south = arrange(maps_ref[1, :, cols], nch + 1)
    mask = arrange(maps_ref[2, :, cols], nch + 2)
    row, col = iota((ext, span), 0), iota((ext, span), 1)
    ww = pltpu.roll(ew, 1, 1)
    if lo == 0:
        ww = jnp.where(col == 0, 0.0, ww)
    sw = -2.0 * south * mask * pltpu.roll(mask, ext - 1, 0)
    for gap in (TILE + HALO - 1, 3 * TILE + HALO - 1) if outer else (ext - HALO - 1,):
        sw = jnp.where(row == gap, 0.0, sw)
    w_buf[0] = ew
    w_buf[1] = ww
    w_buf[2] = sw
    w_buf[3] = pltpu.roll(sw, 1, 0)

    def twice(fields, rounded):
        east, west, south, north = (w_buf[n] for n in range(4))
        out = []
        for v, b in zip(fields, rounded):
            right = pltpu.roll(b, span - 1, 1).astype(F32)
            left = pltpu.roll(b, 1, 1).astype(F32)
            out.append(
                (east * right + west * left)
                + (south * pltpu.roll(v, ext - 1, 0) + north * pltpu.roll(v, 1, 0))
            )
        return out

    def keep(v):
        v = v[:, off : off + width]
        if outer:
            v = jnp.concatenate([v[:TILE], v[2 * TILE : 3 * TILE]], axis=0)
        return v[:SUB].astype(BF16)

    group = 4

    def channels(step, carry):
        chans = [step * group + n for n in range(group)]
        now = [arrange(g_ref[o, :, cols], o) for o in chans]
        prev = None
        for k in range(nterms):
            if k > 0:
                new = twice(now, rounded)
                new = [0.5 * x for x in new] if k == 1 else [x - p for x, p in zip(new, prev)]
                prev, now = now, new
            rounded = [x.astype(BF16) for x in now]
            for o, x in zip(chans, now):
                terms_ref[k * nch + o] = keep(x)
        return carry

    lax.fori_loop(0, nch // group, channels, 0)
    for c in range(0, width, 256):
        x = terms_ref[:, :, c : c + 256].reshape(nterms * nch * SUB, 256)
        y = jnp.dot(mix_ref[: send_ref.shape[0] * SUB], x, preferred_element_type=F32)
        send_ref[:, :, c : c + 256] = y.astype(BF16).reshape(-1, SUB, 256)


def chunk_terms(outer, start, width, g, maps, mix, sent, nterms, beside, waits, cost):
    nch, rows, total = g.shape
    lo, hi = max(0, start - SIDE), min(total, start + width + SIDE)
    ext = 4 * TILE if outer else 3 * TILE
    halo = []
    if outer:
        halo = [
            pltpu.VMEM((beside[1].shape[0] + 2 * TILE, hi - lo), F32),
            pltpu.VMEM((nch + 3, TILE, hi - lo), F32),
        ]
    return pl.pallas_call(
        functools.partial(terms_kernel, outer, start - lo, lo, hi, nterms, len(waits)),
        out_shape=(
            jax.ShapeDtypeStruct((nterms * nch, SUB, width), BF16),
            jax.ShapeDtypeStruct((sent, SUB, width), BF16),
        ),
        in_specs=[ANY] * len(waits) + [VMEM] * (3 + len(beside)),
        out_specs=(VMEM, VMEM),
        scratch_shapes=[pltpu.VMEM((4, ext, hi - lo), F32)] + halo,
        compiler_params=params(20),
        cost_estimate=cost,
    )(*waits, g, maps, mix, *beside)


def weights_kernel(places, f_ref, *refs):
    n = len(places)
    terms, (grad_ref, acc) = refs[:n], refs[n:]
    nt = terms[0].shape[0]
    nin, rows, _ = f_ref.shape
    for m, ((outer, start, width), t_ref) in enumerate(zip(places, terms)):
        x = t_ref[...].reshape(nt * SUB, width)
        f = f_ref[:, :, start : start + width].astype(F32)
        if outer:
            f = jnp.concatenate([f[:, rows - TILE :], f[:, :TILE]], axis=1)
        else:
            f = f[:, TILE : rows - TILE]
        f = f.astype(BF16).reshape(nin * SUB, width)
        y = lax.dot_general(x, f, (((1,), (1,)), ((), ())), preferred_element_type=F32)
        if m == 0:
            acc[...] = y
        else:
            acc[...] += y
    r, c = iota((SUB, nin * SUB), 0), iota((SUB, nin * SUB), 1)
    same = (c % SUB == r).astype(F32)
    kept = jnp.sum(acc[...].reshape(nt, SUB, nin * SUB) * same[None], axis=1)
    pick = (iota((nin * SUB, nin), 0) // SUB == iota((nin * SUB, nin), 1)).astype(F32)
    grad_ref[...] = jnp.dot(
        kept, pick, preferred_element_type=F32, precision=lax.Precision.HIGHEST
    )


def weights(places, terms, f):
    nt = terms[0].shape[0]
    nin = f.shape[0]
    return pl.pallas_call(
        functools.partial(weights_kernel, places),
        out_shape=jax.ShapeDtypeStruct((nt, nin), F32),
        in_specs=[VMEM] * (1 + len(terms)),
        out_specs=VMEM,
        scratch_shapes=[pltpu.VMEM((nt * SUB, nin * SUB), F32)],
        compiler_params=params(24),
        cost_estimate=COST,
    )(f, *terms)


def own_kernel(mix_ref, *refs):
    n = len(refs) // 2
    for t_ref, own_ref in zip(refs[:n], refs[n:]):
        kept = own_ref.shape[0]
        for c in range(0, t_ref.shape[2], UNIT):
            x = t_ref[:, :, c : c + UNIT].reshape(-1, UNIT)
            y = jnp.dot(mix_ref[-kept * SUB :], x, preferred_element_type=F32)
            own_ref[:, :, c : c + UNIT] = y.reshape(kept, SUB, UNIT)


def own_parts(mix, terms, kept):
    return pl.pallas_call(
        own_kernel,
        out_shape=[jax.ShapeDtypeStruct((kept, *t.shape[1:]), F32) for t in terms],
        in_specs=[VMEM] * (1 + len(terms)),
        out_specs=[VMEM] * len(terms),
        compiler_params=params(20),
        cost_estimate=COST,
    )(mix, *terms)


def finish_kernel(start, width, from_i, from_o, own_i, got_i, own_o, got_o, *refs):
    out_ref, mark_ref, buf, sems = refs[-4:]
    mark_ref[...] = jnp.zeros_like(mark_ref)
    copies = []
    for n in range(width // UNIT):
        part = slice(n * UNIT, (n + 1) * UNIT)
        i = slice(from_i + n * UNIT, from_i + (n + 1) * UNIT)
        o = slice(from_o + n * UNIT, from_o + (n + 1) * UNIT)
        inner = own_i[:, :, i] + got_i[:, :, i].astype(F32)
        outer = own_o[:, :, o] + got_o[:, :, o].astype(F32)
        rows = jnp.concatenate([outer[:, TILE:], inner, outer[:, :TILE]], axis=1)
        buf[:, :, part] = rows.astype(BF16)
        copies.append(
            pltpu.make_async_copy(
                buf.at[:, :, pl.ds(n * UNIT, UNIT)],
                out_ref.at[:, :, pl.ds(start + n * UNIT, UNIT)],
                sems.at[n],
            )
        )
        copies[-1].start()
    for c in copies:
        c.wait()


def finish(start, width, inner, outer, out, rows, total):
    kept = outer[2].shape[0]
    extra = () if out is None else (out,)
    return pl.pallas_call(
        functools.partial(finish_kernel, start, width, start - inner[0], start - outer[0]),
        out_shape=(
            jax.ShapeDtypeStruct((kept, rows, total), BF16),
            jax.ShapeDtypeStruct((8, 128), F32),
        ),
        in_specs=[VMEM] * 4 + [ANY] * len(extra),
        out_specs=(ANY, VMEM),
        scratch_shapes=[
            pltpu.VMEM((kept, rows, width), BF16),
            pltpu.SemaphoreType.DMA((width // UNIT,)),
        ],
        input_output_aliases={4: 0} if extra else {},
        compiler_params=params(12),
        cost_estimate=COST,
    )(*inner[1:], *outer[1:], *extra)


def add_kernel(count, scale, *refs):
    values = [r[...] for r in refs[:count]]
    while len(values) > 1:
        values = [a + b for a, b in zip(values[::2], values[1::2])]
    refs[-1][...] = values[0] if scale is None else values[0] / jnp.sqrt(F32(scale))


def add(values, waits, scale=None):
    return pl.pallas_call(
        functools.partial(add_kernel, len(values), scale),
        out_shape=jax.ShapeDtypeStruct(values[0].shape, F32),
        in_specs=[VMEM] * len(values) + [ANY] * len(waits),
        out_specs=VMEM,
        compiler_params=params(4),
        cost_estimate=COST,
    )(*values, *waits)


def sum_over_pix(values, size, waits, scale):
    steps, step = [], 1
    while step < size:
        steps.append((step, 4 if step * 2 < size else 2))
        step *= steps[-1][1]
    value = add(values, waits[0])
    for n, (step, count) in enumerate(steps[1:] + steps[:1]):
        last = n + 1 == len(steps)
        moved = [
            lax.ppermute(value, "pix", [(i, i ^ (x * step)) for i in range(size)])
            for x in range(1, count)
        ]
        wait = waits[n + 1] if n + 1 < len(waits) else ()
        value = add([value, *moved], wait, scale if last else None)
    return value


def per_device(features, grad_out, cheb_weight, east_weight, south_weight, pixel_mask):
    nch, rows, total = grad_out.shape
    nterms, nin, _ = cheb_weight.shape
    size, sides = lax.axis_size("pix"), lax.axis_size("ch")
    part = nin // sides
    mix, g, maps, to_partner, to_other = prepare(
        cheb_weight, grad_out, east_weight, south_weight, pixel_mask, sides
    )
    pieces = []

    def chunks(outer, widths, beside, first):
        start = 0
        for width in widths:
            waits = [pieces[-1][1], *first] if pieces else []
            late = outer and start
            waits += [pieces[0][2]] if late else []
            terms, send = chunk_terms(
                outer, start, width, g, maps, mix, part, nterms, beside, waits,
                LONG if outer and not start else COST,
            )
            got = lax.ppermute(send, "ch", [(i, i ^ 1) for i in range(sides)])
            pieces.append(((outer, start, width), terms, got))
            start += width
            first = ()

    def local(some):
        places, terms, _ = zip(*some)
        return own_parts(mix, terms, part), weights(places, terms, features)

    n = len(INNER)
    chunks(False, INNER, (), ())
    own_inner, grad_inner = local(pieces)
    def swap(x, first):
        pairs = [(i, i + 1) for i in range(first, size - 1, 2) if (i + 1) * rows % total]
        return lax.ppermute(x, "pix", pairs + [(j, i) for i, j in pairs])

    beside = (swap(to_partner, 0), swap(to_other, 1))
    chunks(True, OUTER, beside, (own_inner[0], grad_inner))
    own_outer, grad_outer = local(pieces[n:])
    pieces = [
        (place, own, got) for (place, _, got), own in zip(pieces, (*own_inner, *own_outer))
    ]
    out, marks = None, []
    for (_, at, width), outer_own, outer_got in pieces[n:]:
        for (_, first, span), inner_own, inner_got in pieces[:n]:
            lo, hi = max(at, first), min(at + width, first + span)
            if lo < hi:
                inner = (first, inner_own, inner_got)
                outer = (at, outer_own, outer_got)
                out, mark = finish(lo, hi - lo, inner, outer, out, rows, total)
                marks.append(mark)
    waits = ([got for _, _, got in pieces[:n]], own_outer[:1], marks[-2:-1], marks[-1:])
    grad = sum_over_pix([grad_inner, grad_outer], size, waits, rows * size * total)
    weight_grad = grad.reshape(nterms, nch, nin).transpose(0, 2, 1)
    return out, weight_grad


def solution(mesh):
    return jax.shard_map(
        per_device,
        mesh=mesh,
        in_specs=(
            P(None, "pix", None),
            P("ch", "pix", None),
            P(None, None, "ch"),
            P("pix", None),
            P("pix", None),
            P("pix", None),
        ),
        out_specs=(P("ch", "pix", None), P(None, None, "ch")),
        check_vma=False,
    )
```

```python
import functools

import jax
import jax.numpy as jnp
from jax import lax
from jax.experimental import pallas as pl
from jax.experimental.pallas import tpu as pltpu
from jax.sharding import PartitionSpec as P

HALO = 4
SIDE = 128
SUB = 16
TILE = 8
INNER = (512, 1536)
OUTER = (1024, 1024)
UNIT = 256
PARTS = 4
NEED = 3
ANY = pl.BlockSpec(memory_space=pl.ANY)
HBM = pl.BlockSpec(memory_space=pltpu.HBM)
VMEM = pl.BlockSpec(memory_space=pltpu.VMEM)
F32, BF16 = jnp.float32, jnp.bfloat16


def params(mib):
    return pltpu.CompilerParams(vmem_limit_bytes=mib * 1024 * 1024)


COST = pl.CostEstimate(flops=1, bytes_accessed=1, transcendentals=0)
LONG = pl.CostEstimate(flops=10**10, bytes_accessed=10**8, transcendentals=0)


def iota(shape, dim):
    return lax.broadcasted_iota(jnp.int32, shape, dim)


def dense_rows(n, nch):
    if n < nch:
        return n * NEED, NEED
    before = nch * NEED
    return (before, NEED - 1) if n == nch else (before + (n - nch) * NEED - 1, NEED)


def prepare_kernel(
    sides, w_hbm, g_ref, east_ref, south_ref, mask_ref,
    mix_ref, g_out, maps_out, other_ref, mask_buf, w_ref, dense, sems,
):
    nch = g_out.shape[0]
    some = nch // PARTS
    pairs = [
        (w_hbm, w_ref), (mask_ref, mask_buf), (east_ref, maps_out.at[0]), (south_ref, maps_out.at[1]),
    ]
    for n in range(PARTS):
        part = pl.ds(n * some, some)
        pairs.append((g_ref.at[part], g_out.at[part]))
    copies = [
        pltpu.make_async_copy(src, dst, sems.at[n]) for n, (src, dst) in enumerate(pairs)
    ]
    for c in copies:
        c.start()
    copies[0].wait()
    nterms, nout, nin = w_ref.shape
    rows, cols = nin * SUB, nout * SUB
    part = nin // sides
    first = (lax.axis_index("ch") + 1) * part
    source = lax.rem(iota((rows, nin), 0) // SUB + first, nin)
    left = (source == iota((rows, nin), 1)).astype(BF16)
    right = (iota((nout, cols), 0) == iota((nout, cols), 1) // SUB).astype(BF16)
    keep = iota((rows, cols), 0) % SUB == iota((rows, cols), 1) % SUB
    for k in range(nterms):
        tall = lax.dot_general(
            left, w_ref[k], (((1,), (1,)), ((), ())), preferred_element_type=F32
        ).astype(BF16)
        full = jnp.dot(tall, right, preferred_element_type=F32)
        mix_ref[:, k * cols : (k + 1) * cols] = jnp.where(keep, full, 0.0).astype(BF16)
    for c in copies[1:4]:
        c.wait()
    mask = mask_buf[...].astype(F32)
    height, total = mask.shape
    east = -2.0 * maps_out[0] * mask * pltpu.roll(mask, total - 1, 1)
    maps_out[0] = jnp.where(iota(mask.shape, 1) == total - 1, 0.0, east)
    maps_out[2] = mask
    even = lax.axis_index("pix") % 2 == 0
    for o in range(nch + 3):
        if o < nch and o % some == 0:
            copies[4 + o // some].wait()
        x = g_out[o].astype(F32) if o < nch else maps_out[o - nch]
        head, tail = x[:TILE], x[height - TILE :]
        at, count = dense_rows(o, nch)
        other = jnp.where(even, head, pltpu.roll(tail, count, 0))
        dense[at : at + count] = other[:count]
    other_ref[...] = dense[...].astype(BF16)


def prepare(w, g, east, south, mask, sides):
    nterms, nin, nout = w.shape
    nch, rows, total = g.shape
    dense = (nch + 3) * NEED - 1
    args = (w.transpose(0, 2, 1), g, east, south, mask)
    return pl.pallas_call(
        functools.partial(prepare_kernel, sides),
        out_shape=(
            jax.ShapeDtypeStruct((nin * SUB, nterms * nout * SUB), BF16),
            jax.ShapeDtypeStruct(g.shape, g.dtype),
            jax.ShapeDtypeStruct((3, rows, total), F32),
            jax.ShapeDtypeStruct((dense, total), BF16),
        ),
        in_specs=[HBM] * 5,
        out_specs=[VMEM] * 4,
        scratch_shapes=[
            pltpu.VMEM((rows, total), jnp.int32),
            pltpu.VMEM((nterms, nout, nin), BF16),
            pltpu.VMEM((dense, total), F32),
            pltpu.SemaphoreType.DMA((4 + PARTS,)),
        ],
        compiler_params=params(12),
        cost_estimate=COST,
    )(*(pltpu.with_memory_space_constraint(x, pltpu.HBM) for x in args))


def inner_rows(x):
    rows = x.shape[0]
    low = iota((TILE, x.shape[1]), 0) < HALO
    return jnp.concatenate(
        [x[TILE : rows - TILE], jnp.where(low, x[rows - TILE :], x[:TILE])], axis=0
    )


def outer_rows(x, beside):
    rows = x.shape[0]
    low = iota((TILE, x.shape[1]), 0) < HALO
    return jnp.concatenate(
        [
            x[rows - TILE :], beside, x[:TILE],
            jnp.where(low, x[TILE : 2 * TILE], x[rows - 2 * TILE : rows - TILE]),
        ],
        axis=0,
    )


def terms_kernel(outer, off, lo, hi, nterms, waits, pack, *refs):
    g_ref, maps_ref, mix_ref = refs[waits : waits + 3]
    partner_ref, other_ref = refs[waits + 3 : waits + 5] if outer else (None, None)
    pack_ref = refs[-2] if pack else None
    refs = refs[:-2] + refs[-1:] if pack else refs
    (terms_ref, send_ref, w_buf), tiles = refs[-5:-2] if outer else refs[-3:], refs[-1]
    nch = g_ref.shape[0]
    ext, span = w_buf.shape[1:]
    width = terms_ref.shape[2]
    cols = slice(lo, hi)
    if outer:
        below = 1 - lax.axis_index("pix") % 2
        side = (iota((TILE, span), 0) < HALO).astype(jnp.int32)
        dense = refs[-2]
        count = dense.shape[0] - 2 * TILE
        dense[:TILE] = jnp.zeros((TILE, span), F32)
        dense[TILE : TILE + count] = other_ref[:, cols].astype(F32)
        dense[TILE + count :] = jnp.zeros((TILE, span), F32)
        for n in range(nch + 3):
            at, many = dense_rows(n, nch)
            last, first = dense[at + many : at + many + TILE], dense[TILE + at : 2 * TILE + at]
            tiles[n] = jnp.where(below == 1, last, first)

    def arrange(x, n):
        x = x.astype(F32)
        if outer:
            partner = partner_ref[n, :, cols].astype(F32)
            partner = jnp.concatenate([partner, partner], axis=0)
            return outer_rows(x, jnp.where(side == below, partner, tiles[n]))
        return inner_rows(x)

    ew = arrange(maps_ref[0, :, cols], nch)
    south = arrange(maps_ref[1, :, cols], nch + 1)
    mask = arrange(maps_ref[2, :, cols], nch + 2)
    row, col = iota((ext, span), 0), iota((ext, span), 1)
    ww = pltpu.roll(ew, 1, 1)
    if lo == 0:
        ww = jnp.where(col == 0, 0.0, ww)
    sw = -2.0 * south * mask * pltpu.roll(mask, ext - 1, 0)
    for gap in (TILE + HALO - 1, 3 * TILE + HALO - 1) if outer else (ext - HALO - 1,):
        sw = jnp.where(row == gap, 0.0, sw)
    w_buf[0] = ew
    w_buf[1] = ww
    w_buf[2] = sw
    w_buf[3] = pltpu.roll(sw, 1, 0)

    def twice(fields, rounded):
        east, west, south, north = (w_buf[n] for n in range(4))
        out = []
        for v, b in zip(fields, rounded):
            right = pltpu.roll(b, span - 1, 1).astype(F32)
            left = pltpu.roll(b, 1, 1).astype(F32)
            out.append(
                (east * right + west * left)
                + (south * pltpu.roll(v, ext - 1, 0) + north * pltpu.roll(v, 1, 0))
            )
        return out

    def keep(v):
        v = v[:, off : off + width]
        if outer:
            v = jnp.concatenate([v[:TILE], v[2 * TILE : 3 * TILE]], axis=0)
        return v[:SUB].astype(BF16)

    group = 4

    def channels(step, carry):
        chans = [step * group + n for n in range(group)]
        now = [arrange(g_ref[o, :, cols], o) for o in chans]
        prev = None
        for k in range(nterms):
            if k > 0:
                new = twice(now, rounded)
                new = [0.5 * x for x in new] if k == 1 else [x - p for x, p in zip(new, prev)]
                prev, now = now, new
            rounded = [x.astype(BF16) for x in now]
            for o, x in zip(chans, now):
                terms_ref[k * nch + o] = keep(x)
        return carry

    if pack:
        even = lax.axis_index("pix") % 2 == 0
        for o in range(nch + 3):
            x = g_ref[o].astype(F32) if o < nch else maps_ref[o - nch]
            head, tail = x[:TILE], x[x.shape[0] - TILE :]
            pack_ref[o] = jnp.where(even, tail[TILE - HALO :], head[:HALO]).astype(BF16)
    lax.fori_loop(0, nch // group, channels, 0)
    for c in range(0, width, 256):
        x = terms_ref[:, :, c : c + 256].reshape(nterms * nch * SUB, 256)
        y = jnp.dot(mix_ref[: send_ref.shape[0] * SUB], x, preferred_element_type=F32)
        send_ref[:, :, c : c + 256] = y.astype(BF16).reshape(-1, SUB, 256)


def chunk_terms(outer, start, width, g, maps, mix, sent, nterms, beside, waits, cost):
    nch, rows, total = g.shape
    lo, hi = max(0, start - SIDE), min(total, start + width + SIDE)
    ext = 4 * TILE if outer else 3 * TILE
    pack = not waits
    packed = [jax.ShapeDtypeStruct((nch + 3, HALO, total), BF16)] if pack else []
    halo = []
    if outer:
        halo = [
            pltpu.VMEM((beside[1].shape[0] + 2 * TILE, hi - lo), F32),
            pltpu.VMEM((nch + 3, TILE, hi - lo), F32),
        ]
    return pl.pallas_call(
        functools.partial(terms_kernel, outer, start - lo, lo, hi, nterms, len(waits), pack),
        out_shape=(
            jax.ShapeDtypeStruct((nterms * nch, SUB, width), BF16),
            jax.ShapeDtypeStruct((sent, SUB, width), BF16),
            *packed,
        ),
        in_specs=[ANY] * len(waits) + [VMEM] * (3 + len(beside)),
        out_specs=(VMEM,) * (2 + pack),
        scratch_shapes=[pltpu.VMEM((4, ext, hi - lo), F32)] + halo,
        compiler_params=params(20),
        cost_estimate=cost,
    )(*waits, g, maps, mix, *beside)


def weights_kernel(places, f_ref, *refs):
    n = len(places)
    terms, (grad_ref, acc) = refs[:n], refs[n:]
    nt = terms[0].shape[0]
    nin, rows, _ = f_ref.shape
    for m, ((outer, start, width), t_ref) in enumerate(zip(places, terms)):
        x = t_ref[...].reshape(nt * SUB, width)
        f = f_ref[:, :, start : start + width].astype(F32)
        if outer:
            f = jnp.concatenate([f[:, rows - TILE :], f[:, :TILE]], axis=1)
        else:
            f = f[:, TILE : rows - TILE]
        f = f.astype(BF16).reshape(nin * SUB, width)
        y = lax.dot_general(x, f, (((1,), (1,)), ((), ())), preferred_element_type=F32)
        if m == 0:
            acc[...] = y
        else:
            acc[...] += y
    r, c = iota((SUB, nin * SUB), 0), iota((SUB, nin * SUB), 1)
    same = (c % SUB == r).astype(F32)
    kept = jnp.sum(acc[...].reshape(nt, SUB, nin * SUB) * same[None], axis=1)
    pick = (iota((nin * SUB, nin), 0) // SUB == iota((nin * SUB, nin), 1)).astype(F32)
    grad_ref[...] = jnp.dot(
        kept, pick, preferred_element_type=F32, precision=lax.Precision.HIGHEST
    )


def weights(places, terms, f):
    nt = terms[0].shape[0]
    nin = f.shape[0]
    return pl.pallas_call(
        functools.partial(weights_kernel, places),
        out_shape=jax.ShapeDtypeStruct((nt, nin), F32),
        in_specs=[VMEM] * (1 + len(terms)),
        out_specs=VMEM,
        scratch_shapes=[pltpu.VMEM((nt * SUB, nin * SUB), F32)],
        compiler_params=params(24),
        cost_estimate=COST,
    )(f, *terms)


def own_kernel(mix_ref, *refs):
    n = len(refs) // 2
    for t_ref, own_ref in zip(refs[:n], refs[n:]):
        kept = own_ref.shape[0]
        for c in range(0, t_ref.shape[2], UNIT):
            x = t_ref[:, :, c : c + UNIT].reshape(-1, UNIT)
            y = jnp.dot(mix_ref[-kept * SUB :], x, preferred_element_type=F32)
            own_ref[:, :, c : c + UNIT] = y.reshape(kept, SUB, UNIT)


def own_parts(mix, terms, kept):
    return pl.pallas_call(
        own_kernel,
        out_shape=[jax.ShapeDtypeStruct((kept, *t.shape[1:]), F32) for t in terms],
        in_specs=[VMEM] * (1 + len(terms)),
        out_specs=[VMEM] * len(terms),
        compiler_params=params(20),
        cost_estimate=COST,
    )(mix, *terms)


def finish_kernel(start, width, from_i, from_o, own_i, got_i, own_o, got_o, *refs):
    out_ref, mark_ref, buf, sems = refs[-4:]
    mark_ref[...] = jnp.zeros_like(mark_ref)
    copies = []
    for n in range(width // UNIT):
        part = slice(n * UNIT, (n + 1) * UNIT)
        i = slice(from_i + n * UNIT, from_i + (n + 1) * UNIT)
        o = slice(from_o + n * UNIT, from_o + (n + 1) * UNIT)
        inner = own_i[:, :, i] + got_i[:, :, i].astype(F32)
        outer = own_o[:, :, o] + got_o[:, :, o].astype(F32)
        rows = jnp.concatenate([outer[:, TILE:], inner, outer[:, :TILE]], axis=1)
        buf[:, :, part] = rows.astype(BF16)
        copies.append(
            pltpu.make_async_copy(
                buf.at[:, :, pl.ds(n * UNIT, UNIT)],
                out_ref.at[:, :, pl.ds(start + n * UNIT, UNIT)],
                sems.at[n],
            )
        )
        copies[-1].start()
    for c in copies:
        c.wait()


def finish(start, width, inner, outer, out, rows, total):
    kept = outer[2].shape[0]
    extra = () if out is None else (out,)
    return pl.pallas_call(
        functools.partial(finish_kernel, start, width, start - inner[0], start - outer[0]),
        out_shape=(
            jax.ShapeDtypeStruct((kept, rows, total), BF16),
            jax.ShapeDtypeStruct((8, 128), F32),
        ),
        in_specs=[VMEM] * 4 + [ANY] * len(extra),
        out_specs=(ANY, VMEM),
        scratch_shapes=[
            pltpu.VMEM((kept, rows, width), BF16),
            pltpu.SemaphoreType.DMA((width // UNIT,)),
        ],
        input_output_aliases={4: 0} if extra else {},
        compiler_params=params(12),
        cost_estimate=COST,
    )(*inner[1:], *outer[1:], *extra)


def add_kernel(count, scale, *refs):
    values = [r[...] for r in refs[:count]]
    while len(values) > 1:
        values = [a + b for a, b in zip(values[::2], values[1::2])]
    refs[-1][...] = values[0] if scale is None else values[0] / jnp.sqrt(F32(scale))


def add(values, waits, scale=None):
    return pl.pallas_call(
        functools.partial(add_kernel, len(values), scale),
        out_shape=jax.ShapeDtypeStruct(values[0].shape, F32),
        in_specs=[VMEM] * len(values) + [ANY] * len(waits),
        out_specs=VMEM,
        compiler_params=params(4),
        cost_estimate=COST,
    )(*values, *waits)


def sum_over_pix(values, size, waits, scale):
    steps, step = [], 1
    while step < size:
        steps.append((step, 4 if step * 2 < size else 2))
        step *= steps[-1][1]
    value = add(values, waits[0])
    for n, (step, count) in enumerate(steps[1:] + steps[:1]):
        last = n + 1 == len(steps)
        moved = [
            lax.ppermute(value, "pix", [(i, i ^ (x * step)) for i in range(size)])
            for x in range(1, count)
        ]
        wait = waits[n + 1] if n + 1 < len(waits) else ()
        value = add([value, *moved], wait, scale if last else None)
    return value


def per_device(features, grad_out, cheb_weight, east_weight, south_weight, pixel_mask):
    nch, rows, total = grad_out.shape
    nterms, nin, _ = cheb_weight.shape
    size, sides = lax.axis_size("pix"), lax.axis_size("ch")
    part = nin // sides
    mix, g, maps, to_other = prepare(
        cheb_weight, grad_out, east_weight, south_weight, pixel_mask, sides
    )
    pieces, to_partner = [], []

    def chunks(outer, widths, beside, first):
        start = 0
        for width in widths:
            waits = [pieces[-1][1], *first] if pieces else []
            late = outer and start
            waits += [pieces[0][2]] if late else []
            terms, send, *packed = chunk_terms(
                outer, start, width, g, maps, mix, part, nterms, beside, waits,
                LONG if outer and not start or not outer and start else COST,
            )
            got = lax.ppermute(send, "ch", [(i, i ^ 1) for i in range(sides)])
            pieces.append(((outer, start, width), terms, got))
            to_partner.extend(packed)
            start += width
            first = ()

    def local(some):
        places, terms, _ = zip(*some)
        return own_parts(mix, terms, part), weights(places, terms, features)

    n = len(INNER)
    chunks(False, INNER, (), ())
    own_inner, grad_inner = local(pieces)
    def swap(x, first):
        pairs = [(i, i + 1) for i in range(first, size - 1, 2) if (i + 1) * rows % total]
        return lax.ppermute(x, "pix", pairs + [(j, i) for i, j in pairs])

    beside = (swap(to_partner[0], 0), swap(to_other, 1))
    chunks(True, OUTER, beside, (own_inner[0], grad_inner))
    own_outer, grad_outer = local(pieces[n:])
    pieces = [
        (place, own, got) for (place, _, got), own in zip(pieces, (*own_inner, *own_outer))
    ]
    out, marks = None, []
    for (_, at, width), outer_own, outer_got in pieces[n:]:
        for (_, first, span), inner_own, inner_got in pieces[:n]:
            lo, hi = max(at, first), min(at + width, first + span)
            if lo < hi:
                inner = (first, inner_own, inner_got)
                outer = (at, outer_own, outer_got)
                out, mark = finish(lo, hi - lo, inner, outer, out, rows, total)
                marks.append(mark)
    waits = ([got for _, _, got in pieces[:n]], own_outer[:1], marks[-2:-1], marks[-1:])
    grad = sum_over_pix([grad_inner, grad_outer], size, waits, rows * size * total)
    weight_grad = grad.reshape(nterms, nch, nin).transpose(0, 2, 1)
    return out, weight_grad


def solution(mesh):
    return jax.shard_map(
        per_device,
        mesh=mesh,
        in_specs=(
            P(None, "pix", None),
            P("ch", "pix", None),
            P(None, None, "ch"),
            P("pix", None),
            P("pix", None),
            P("pix", None),
        ),
        out_specs=(P("ch", "pix", None), P(None, None, "ch")),
        check_vma=False,
    )
```

```python
import functools

import jax
import jax.numpy as jnp
from jax import lax
from jax.experimental import pallas as pl
from jax.experimental.pallas import tpu as pltpu
from jax.sharding import PartitionSpec as P

HALO = 4
SIDE = 128
SUB = 16
TILE = 8
INNER = (512, 1536)
OUTER = (1024, 1024)
UNIT = 256
PARTS = 4
NEED = 3
ANY = pl.BlockSpec(memory_space=pl.ANY)
HBM = pl.BlockSpec(memory_space=pltpu.HBM)
VMEM = pl.BlockSpec(memory_space=pltpu.VMEM)
F32, BF16 = jnp.float32, jnp.bfloat16


def params(mib):
    return pltpu.CompilerParams(vmem_limit_bytes=mib * 1024 * 1024)


COST = pl.CostEstimate(flops=1, bytes_accessed=1, transcendentals=0)
LONG = pl.CostEstimate(flops=10**10, bytes_accessed=10**8, transcendentals=0)


def iota(shape, dim):
    return lax.broadcasted_iota(jnp.int32, shape, dim)


def dense_rows(n, nch):
    if n < nch:
        return n * NEED, NEED
    before = nch * NEED
    return (before, NEED - 1) if n == nch else (before + (n - nch) * NEED - 1, NEED)


def prepare_kernel(
    sides, w_hbm, g_ref, east_ref, south_ref, mask_ref,
    mix_ref, g_out, maps_out, partner_ref, other_ref, mask_buf, w_ref, dense, sems,
):
    nch = g_out.shape[0]
    some = nch // PARTS
    pairs = [
        (w_hbm, w_ref), (mask_ref, mask_buf), (east_ref, maps_out.at[0]), (south_ref, maps_out.at[1]),
    ]
    for n in range(PARTS):
        part = pl.ds(n * some, some)
        pairs.append((g_ref.at[part], g_out.at[part]))
    copies = [
        pltpu.make_async_copy(src, dst, sems.at[n]) for n, (src, dst) in enumerate(pairs)
    ]
    for c in copies:
        c.start()
    copies[0].wait()
    nterms, nout, nin = w_ref.shape
    rows, cols = nin * SUB, nout * SUB
    part = nin // sides
    first = (lax.axis_index("ch") + 1) * part
    source = lax.rem(iota((rows, nin), 0) // SUB + first, nin)
    left = (source == iota((rows, nin), 1)).astype(BF16)
    right = (iota((nout, cols), 0) == iota((nout, cols), 1) // SUB).astype(BF16)
    keep = iota((rows, cols), 0) % SUB == iota((rows, cols), 1) % SUB
    for k in range(nterms):
        tall = lax.dot_general(
            left, w_ref[k], (((1,), (1,)), ((), ())), preferred_element_type=F32
        ).astype(BF16)
        full = jnp.dot(tall, right, preferred_element_type=F32)
        mix_ref[:, k * cols : (k + 1) * cols] = jnp.where(keep, full, 0.0).astype(BF16)
    for c in copies[1:4]:
        c.wait()
    mask = mask_buf[...].astype(F32)
    height, total = mask.shape
    east = -2.0 * maps_out[0] * mask * pltpu.roll(mask, total - 1, 1)
    maps_out[0] = jnp.where(iota(mask.shape, 1) == total - 1, 0.0, east)
    maps_out[2] = mask
    even = lax.axis_index("pix") % 2 == 0
    for o in range(nch + 3):
        if o < nch and o % some == 0:
            copies[4 + o // some].wait()
        x = g_out[o].astype(F32) if o < nch else maps_out[o - nch]
        head, tail = x[:TILE], x[height - TILE :]
        partner = jnp.where(even, tail[TILE - HALO :], head[:HALO])
        partner_ref[o] = partner.astype(BF16)
        at, count = dense_rows(o, nch)
        other = jnp.where(even, head, pltpu.roll(tail, count, 0))
        dense[at : at + count] = other[:count]
    other_ref[...] = dense[...].astype(BF16)


def prepare(w, g, east, south, mask, sides):
    nterms, nin, nout = w.shape
    nch, rows, total = g.shape
    dense = (nch + 3) * NEED - 1
    args = (w.transpose(0, 2, 1), g, east, south, mask)
    return pl.pallas_call(
        functools.partial(prepare_kernel, sides),
        out_shape=(
            jax.ShapeDtypeStruct((nin * SUB, nterms * nout * SUB), BF16),
            jax.ShapeDtypeStruct(g.shape, g.dtype),
            jax.ShapeDtypeStruct((3, rows, total), F32),
            jax.ShapeDtypeStruct((nch + 3, HALO, total), BF16),
            jax.ShapeDtypeStruct((dense, total), BF16),
        ),
        in_specs=[HBM] * 5,
        out_specs=[VMEM] * 5,
        scratch_shapes=[
            pltpu.VMEM((rows, total), jnp.int32),
            pltpu.VMEM((nterms, nout, nin), BF16),
            pltpu.VMEM((dense, total), F32),
            pltpu.SemaphoreType.DMA((4 + PARTS,)),
        ],
        compiler_params=params(12),
        cost_estimate=COST,
    )(*(pltpu.with_memory_space_constraint(x, pltpu.HBM) for x in args))


def inner_rows(x):
    rows = x.shape[0]
    low = iota((TILE, x.shape[1]), 0) < HALO
    return jnp.concatenate(
        [x[TILE : rows - TILE], jnp.where(low, x[rows - TILE :], x[:TILE])], axis=0
    )


def outer_rows(x, beside):
    rows = x.shape[0]
    low = iota((TILE, x.shape[1]), 0) < HALO
    return jnp.concatenate(
        [
            x[rows - TILE :], beside, x[:TILE],
            jnp.where(low, x[TILE : 2 * TILE], x[rows - 2 * TILE : rows - TILE]),
        ],
        axis=0,
    )


def terms_kernel(outer, off, lo, hi, nterms, waits, *refs):
    g_ref, maps_ref, mix_ref = refs[waits : waits + 3]
    partner_ref, other_ref = refs[waits + 3 : waits + 5] if outer else (None, None)
    (terms_ref, send_ref, w_buf), tiles = refs[-5:-2] if outer else refs[-3:], refs[-1]
    nch = g_ref.shape[0]
    ext, span = w_buf.shape[1:]
    width = terms_ref.shape[2]
    cols = slice(lo, hi)
    if outer:
        below = 1 - lax.axis_index("pix") % 2
        side = (iota((TILE, span), 0) < HALO).astype(jnp.int32)
        dense = refs[-2]
        count = dense.shape[0] - 2 * TILE
        dense[:TILE] = jnp.zeros((TILE, span), F32)
        dense[TILE : TILE + count] = other_ref[:, cols].astype(F32)
        dense[TILE + count :] = jnp.zeros((TILE, span), F32)
        for n in range(nch + 3):
            at, many = dense_rows(n, nch)
            last, first = dense[at + many : at + many + TILE], dense[TILE + at : 2 * TILE + at]
            tiles[n] = jnp.where(below == 1, last, first)

    def arrange(x, n):
        x = x.astype(F32)
        if outer:
            partner = partner_ref[n, :, cols].astype(F32)
            partner = jnp.concatenate([partner, partner], axis=0)
            return outer_rows(x, jnp.where(side == below, partner, tiles[n]))
        return inner_rows(x)

    ew = arrange(maps_ref[0, :, cols], nch)
    south = arrange(maps_ref[1, :, cols], nch + 1)
    mask = arrange(maps_ref[2, :, cols], nch + 2)
    row, col = iota((ext, span), 0), iota((ext, span), 1)
    ww = pltpu.roll(ew, 1, 1)
    if lo == 0:
        ww = jnp.where(col == 0, 0.0, ww)
    sw = -2.0 * south * mask * pltpu.roll(mask, ext - 1, 0)
    for gap in (TILE + HALO - 1, 3 * TILE + HALO - 1) if outer else (ext - HALO - 1,):
        sw = jnp.where(row == gap, 0.0, sw)
    w_buf[0] = ew
    w_buf[1] = ww
    w_buf[2] = sw
    w_buf[3] = pltpu.roll(sw, 1, 0)

    def twice(fields, rounded):
        east, west, south, north = (w_buf[n] for n in range(4))
        out = []
        for v, b in zip(fields, rounded):
            right = pltpu.roll(b, span - 1, 1).astype(F32)
            left = pltpu.roll(b, 1, 1).astype(F32)
            out.append(
                (east * right + west * left)
                + (south * pltpu.roll(v, ext - 1, 0) + north * pltpu.roll(v, 1, 0))
            )
        return out

    def keep(v):
        v = v[:, off : off + width]
        if outer:
            v = jnp.concatenate([v[:TILE], v[2 * TILE : 3 * TILE]], axis=0)
        return v[:SUB].astype(BF16)

    group = 8

    def channels(step, carry):
        chans = [step * group + n for n in range(group)]
        now = [arrange(g_ref[o, :, cols], o) for o in chans]
        prev = None
        for k in range(nterms):
            if k > 0:
                new = twice(now, rounded)
                new = [0.5 * x for x in new] if k == 1 else [x - p for x, p in zip(new, prev)]
                prev, now = now, new
            rounded = [x.astype(BF16) for x in now]
            for o, x in zip(chans, now):
                terms_ref[k * nch + o] = keep(x)
        return carry

    lax.fori_loop(0, nch // group, channels, 0)
    for c in range(0, width, 256):
        x = terms_ref[:, :, c : c + 256].reshape(nterms * nch * SUB, 256)
        y = jnp.dot(mix_ref[: send_ref.shape[0] * SUB], x, preferred_element_type=F32)
        send_ref[:, :, c : c + 256] = y.astype(BF16).reshape(-1, SUB, 256)


def chunk_terms(outer, start, width, g, maps, mix, sent, nterms, beside, waits, cost):
    nch, rows, total = g.shape
    lo, hi = max(0, start - SIDE), min(total, start + width + SIDE)
    ext = 4 * TILE if outer else 3 * TILE
    halo = []
    if outer:
        halo = [
            pltpu.VMEM((beside[1].shape[0] + 2 * TILE, hi - lo), F32),
            pltpu.VMEM((nch + 3, TILE, hi - lo), F32),
        ]
    return pl.pallas_call(
        functools.partial(terms_kernel, outer, start - lo, lo, hi, nterms, len(waits)),
        out_shape=(
            jax.ShapeDtypeStruct((nterms * nch, SUB, width), BF16),
            jax.ShapeDtypeStruct((sent, SUB, width), BF16),
        ),
        in_specs=[ANY] * len(waits) + [VMEM] * (3 + len(beside)),
        out_specs=(VMEM, VMEM),
        scratch_shapes=[pltpu.VMEM((4, ext, hi - lo), F32)] + halo,
        compiler_params=params(20),
        cost_estimate=cost,
    )(*waits, g, maps, mix, *beside)


def weights_kernel(places, f_ref, *refs):
    n = len(places)
    terms, (grad_ref, acc) = refs[:n], refs[n:]
    nt = terms[0].shape[0]
    nin, rows, _ = f_ref.shape
    for m, ((outer, start, width), t_ref) in enumerate(zip(places, terms)):
        x = t_ref[...].reshape(nt * SUB, width)
        f = f_ref[:, :, start : start + width].astype(F32)
        if outer:
            f = jnp.concatenate([f[:, rows - TILE :], f[:, :TILE]], axis=1)
        else:
            f = f[:, TILE : rows - TILE]
        f = f.astype(BF16).reshape(nin * SUB, width)
        y = lax.dot_general(x, f, (((1,), (1,)), ((), ())), preferred_element_type=F32)
        if m == 0:
            acc[...] = y
        else:
            acc[...] += y
    r, c = iota((SUB, nin * SUB), 0), iota((SUB, nin * SUB), 1)
    same = (c % SUB == r).astype(F32)
    kept = jnp.sum(acc[...].reshape(nt, SUB, nin * SUB) * same[None], axis=1)
    pick = (iota((nin * SUB, nin), 0) // SUB == iota((nin * SUB, nin), 1)).astype(F32)
    grad_ref[...] = jnp.dot(
        kept, pick, preferred_element_type=F32, precision=lax.Precision.HIGHEST
    )


def weights(places, terms, f):
    nt = terms[0].shape[0]
    nin = f.shape[0]
    return pl.pallas_call(
        functools.partial(weights_kernel, places),
        out_shape=jax.ShapeDtypeStruct((nt, nin), F32),
        in_specs=[VMEM] * (1 + len(terms)),
        out_specs=VMEM,
        scratch_shapes=[pltpu.VMEM((nt * SUB, nin * SUB), F32)],
        compiler_params=params(24),
        cost_estimate=COST,
    )(f, *terms)


def own_kernel(mix_ref, *refs):
    n = len(refs) // 2
    for t_ref, own_ref in zip(refs[:n], refs[n:]):
        kept = own_ref.shape[0]
        for c in range(0, t_ref.shape[2], UNIT):
            x = t_ref[:, :, c : c + UNIT].reshape(-1, UNIT)
            y = jnp.dot(mix_ref[-kept * SUB :], x, preferred_element_type=F32)
            own_ref[:, :, c : c + UNIT] = y.reshape(kept, SUB, UNIT)


def own_parts(mix, terms, kept):
    return pl.pallas_call(
        own_kernel,
        out_shape=[jax.ShapeDtypeStruct((kept, *t.shape[1:]), F32) for t in terms],
        in_specs=[VMEM] * (1 + len(terms)),
        out_specs=[VMEM] * len(terms),
        compiler_params=params(20),
        cost_estimate=COST,
    )(mix, *terms)


def finish_kernel(start, width, from_i, from_o, own_i, got_i, own_o, got_o, *refs):
    out_ref, mark_ref, buf, sems = refs[-4:]
    mark_ref[...] = jnp.zeros_like(mark_ref)
    copies = []
    for n in range(width // UNIT):
        part = slice(n * UNIT, (n + 1) * UNIT)
        i = slice(from_i + n * UNIT, from_i + (n + 1) * UNIT)
        o = slice(from_o + n * UNIT, from_o + (n + 1) * UNIT)
        inner = own_i[:, :, i] + got_i[:, :, i].astype(F32)
        outer = own_o[:, :, o] + got_o[:, :, o].astype(F32)
        rows = jnp.concatenate([outer[:, TILE:], inner, outer[:, :TILE]], axis=1)
        buf[:, :, part] = rows.astype(BF16)
        copies.append(
            pltpu.make_async_copy(
                buf.at[:, :, pl.ds(n * UNIT, UNIT)],
                out_ref.at[:, :, pl.ds(start + n * UNIT, UNIT)],
                sems.at[n],
            )
        )
        copies[-1].start()
    for c in copies:
        c.wait()


def finish(start, width, inner, outer, out, rows, total):
    kept = outer[2].shape[0]
    extra = () if out is None else (out,)
    return pl.pallas_call(
        functools.partial(finish_kernel, start, width, start - inner[0], start - outer[0]),
        out_shape=(
            jax.ShapeDtypeStruct((kept, rows, total), BF16),
            jax.ShapeDtypeStruct((8, 128), F32),
        ),
        in_specs=[VMEM] * 4 + [ANY] * len(extra),
        out_specs=(ANY, VMEM),
        scratch_shapes=[
            pltpu.VMEM((kept, rows, width), BF16),
            pltpu.SemaphoreType.DMA((width // UNIT,)),
        ],
        input_output_aliases={4: 0} if extra else {},
        compiler_params=params(12),
        cost_estimate=COST,
    )(*inner[1:], *outer[1:], *extra)


def add_kernel(count, scale, *refs):
    values = [r[...] for r in refs[:count]]
    while len(values) > 1:
        values = [a + b for a, b in zip(values[::2], values[1::2])]
    refs[-1][...] = values[0] if scale is None else values[0] / jnp.sqrt(F32(scale))


def add(values, waits, scale=None):
    return pl.pallas_call(
        functools.partial(add_kernel, len(values), scale),
        out_shape=jax.ShapeDtypeStruct(values[0].shape, F32),
        in_specs=[VMEM] * len(values) + [ANY] * len(waits),
        out_specs=VMEM,
        compiler_params=params(4),
        cost_estimate=COST,
    )(*values, *waits)


def sum_over_pix(values, size, waits, scale):
    steps, step = [], 1
    while step < size:
        steps.append((step, 4 if step * 2 < size else 2))
        step *= steps[-1][1]
    value = add(values, waits[0])
    for n, (step, count) in enumerate(steps[1:] + steps[:1]):
        last = n + 1 == len(steps)
        moved = [
            lax.ppermute(value, "pix", [(i, i ^ (x * step)) for i in range(size)])
            for x in range(1, count)
        ]
        wait = waits[n + 1] if n + 1 < len(waits) else ()
        value = add([value, *moved], wait, scale if last else None)
    return value


def per_device(features, grad_out, cheb_weight, east_weight, south_weight, pixel_mask):
    nch, rows, total = grad_out.shape
    nterms, nin, _ = cheb_weight.shape
    size, sides = lax.axis_size("pix"), lax.axis_size("ch")
    part = nin // sides
    mix, g, maps, to_partner, to_other = prepare(
        cheb_weight, grad_out, east_weight, south_weight, pixel_mask, sides
    )
    pieces = []

    def chunks(outer, widths, beside, first):
        start = 0
        for width in widths:
            waits = [pieces[-1][1], *first] if pieces else []
            late = outer and start
            waits += [pieces[0][2]] if late else []
            terms, send = chunk_terms(
                outer, start, width, g, maps, mix, part, nterms, beside, waits,
                LONG if outer and not start else COST,
            )
            got = lax.ppermute(send, "ch", [(i, i ^ 1) for i in range(sides)])
            pieces.append(((outer, start, width), terms, got))
            start += width
            first = ()

    def local(some):
        places, terms, _ = zip(*some)
        return own_parts(mix, terms, part), weights(places, terms, features)

    n = len(INNER)
    chunks(False, INNER, (), ())
    own_inner, grad_inner = local(pieces)
    def swap(x, first):
        pairs = [(i, i + 1) for i in range(first, size - 1, 2) if (i + 1) * rows % total]
        return lax.ppermute(x, "pix", pairs + [(j, i) for i, j in pairs])

    beside = (swap(to_partner, 0), swap(to_other, 1))
    chunks(True, OUTER, beside, (own_inner[0], grad_inner))
    own_outer, grad_outer = local(pieces[n:])
    pieces = [
        (place, own, got) for (place, _, got), own in zip(pieces, (*own_inner, *own_outer))
    ]
    out, marks = None, []
    for (_, at, width), outer_own, outer_got in pieces[n:]:
        for (_, first, span), inner_own, inner_got in pieces[:n]:
            lo, hi = max(at, first), min(at + width, first + span)
            if lo < hi:
                inner = (first, inner_own, inner_got)
                outer = (at, outer_own, outer_got)
                out, mark = finish(lo, hi - lo, inner, outer, out, rows, total)
                marks.append(mark)
    waits = ([got for _, _, got in pieces[:n]], own_outer[:1], marks[-2:-1], marks[-1:])
    grad = sum_over_pix([grad_inner, grad_outer], size, waits, rows * size * total)
    weight_grad = grad.reshape(nterms, nch, nin).transpose(0, 2, 1)
    return out, weight_grad


def solution(mesh):
    return jax.shard_map(
        per_device,
        mesh=mesh,
        in_specs=(
            P(None, "pix", None),
            P("ch", "pix", None),
            P(None, None, "ch"),
            P("pix", None),
            P("pix", None),
            P("pix", None),
        ),
        out_specs=(P("ch", "pix", None), P(None, None, "ch")),
        check_vma=False,
    )
```
